256 devices in a mesh: gx: 16 (over y, x), gy: 8 (over z), gz: 2 (over core).
Axes of the slice: x: 4, y: 4, z: 8, core: 2. Of those that a mesh axis runs over, the one named last changes fastest.
Arguments:
- right_side: float32 [16, 1024, 1024], P('gz', 'gx', 'gy'), may hold values from -6 to 6
- permeability: float32 [16, 1024, 1024], P('gz', 'gx', 'gy'), may hold values from 0.05 to 50
- storage: float32 [16, 1024, 1024], P('gz', 'gx', 'gy'), may hold values from 0.05 to 0.5
- deflation: float32 [8, 16, 1024, 1024], P(None, 'gz', 'gx', 'gy'), may hold values from -0.0234375 to 0.0234375
- coarse_inverse: float32 [2048, 2048], P('gx'), as said below
- owners: int32 [2, 16, 8, 8], P('gz', 'gx', 'gy'), may hold values from 0 to 2047, as said below
- margin: int32 [2, 16, 8, 6], P('gz', 'gx', 'gy'), may hold values from 0 to 1
Outputs:
- solution: float32 [16, 1024, 1024], P('gz', 'gx', 'gy')
- residual: float32 [16, 1024, 1024], P('gz', 'gx', 'gy')
The draws below stay inside these ranges and needn't reach their ends.
Inputs may be any that keep to these rules, and one draw needn't show every extreme that they name: `coarse_inverse`: symmetric and positive definite. `owners`: every coarse index appears exactly once.
All inputs are finite; a program needn't handle non-finite values.
Results may differ from the reference program's by a relative error of at most 0.0003.
Values sent between devices are 32-bit elements; how exact they have to be, the bound alone decides.
A program may use at most 128 MiB of HBM per device.

```python
import math
import jax
import jax.numpy as jnp
from jax import lax

CZ = 8
CX = 64
CY = 128
NV = 8
SWEEPS = 2
ITERS = 4
NBZ = 2
NBX = 16
NBY = 8
NZ = 16
NX = 1024
NY = 1024
COARSE = 2048
N_GX = 16
N_GY = 8
N_GZ = 2


def draw_coarse_inverse(key, part):
    noise_key = jax.random.fold_in(key, 11)
    diag_key = jax.random.fold_in(key, 12)
    noise_part = jax.random.normal(noise_key, (COARSE, COARSE), jnp.float32) * (0.4 / math.sqrt(2.0 * COARSE))
    diagonal = 1.0 + 0.2 * jax.random.uniform(diag_key, (COARSE,), jnp.float32)
    matrix = noise_part + noise_part.T + jnp.diag(diagonal)
    return matrix * (0.2 * math.sqrt(CZ * CX * CY / NV))


def draw_owners(key, part):
    shuffled = jax.random.permutation(jax.random.fold_in(key, 21), COARSE)
    return shuffled.astype(jnp.int32).reshape(NBZ, NBX, NBY, NV)


def draw_margin(key, part):
    depth_draw = jax.random.randint(jax.random.fold_in(key, 31), (NBZ, NBX, NBY, 6), 0, 2).astype(jnp.int32)
    depth_draw = depth_draw.at[0, 0, 0, 0].set(1)
    return depth_draw.at[0, 0, 0, 1].set(0)


def block_levels(key, extent, split, smallest, high):
    gain, own = 1.0, jax.random.fold_in(key, 6)
    for dim, shards_of in split:
        steps = jnp.exp(jax.random.uniform(jax.random.fold_in(own, dim), (shards_of,), jnp.float32, smallest / len(split), high / len(split)))
        gain = gain * jnp.repeat(steps, extent[dim] // shards_of).reshape([-1 if axis == dim else 1 for axis in range(len(extent))])
    return gain


def normal_values(key, shape, scale, limit, cuts=(), kind=jnp.bfloat16):
    entries = jax.random.normal(key, shape, jnp.float32) * scale
    if len(cuts) > 0:
        entries = block_levels(key, shape, cuts, -0.22, 0.18) * entries
    return jnp.clip(entries, min=-limit, max=limit).astype(kind)


def setup_inputs(seed: int = 0) -> dict:
    splits = jax.random.split(jax.random.key(seed), 8)
    return {
        "right_side": normal_values(splits[0], (NZ, NX, NY), 1.0, 6.0, ((0, 2), (1, 16), (2, 8)), jnp.float32),
        "permeability": jnp.clip(jnp.exp(math.log(50.0) - 6.9077553 * jax.random.uniform(splits[1], (NZ, NX, NY), jnp.float32) ** block_levels(splits[1], (NZ, NX, NY), ((0, 2), (1, 16), (2, 8)), -0.2, 0.2)), 0.05, 50.0),
        "storage": jnp.clip(jnp.exp(math.log(0.5) - 2.3025851 * jax.random.uniform(splits[2], (NZ, NX, NY), jnp.float32) ** block_levels(splits[2], (NZ, NX, NY), ((0, 2), (1, 16), (2, 8)), -0.2, 0.2)), 0.05, 0.5),
        "deflation": normal_values(splits[3], (NV, NZ, NX, NY), (CZ * CX * CY) ** -0.5, 0.0234375, ((1, 2), (2, 16), (3, 8)), jnp.float32),
        "coarse_inverse": draw_coarse_inverse(jax.random.fold_in(splits[7], 71), 0),
        "owners": draw_owners(jax.random.fold_in(splits[7], 71), 0),
        "margin": draw_margin(jax.random.fold_in(splits[7], 71), 0),
    }


RELAXATION = 0.7
PRECISE = lax.Precision.HIGHEST


def conduct(first_perm, second_perm):
    return 2.0 * first_perm * second_perm / jnp.maximum(first_perm + second_perm, 0.05)


def neighbour(padded, dimension, offset):
    starts = [1, 1, 1]
    starts[dimension] = 1 + offset
    limits = [starts[0] + padded.shape[0] - 2, starts[1] + padded.shape[1] - 2, starts[2] + padded.shape[2] - 2]
    return lax.slice(padded, starts, limits)


def diagonal_of(perm_pad, storage_in):
    perm_center = neighbour(perm_pad, 0, 0)
    diagonal = storage_in
    for dimension in range(3):
        for offset in (-1, 1):
            diagonal = diagonal + conduct(perm_center, neighbour(perm_pad, dimension, offset))
    return diagonal


def stencil(padded, perm_pad, storage_in):
    center = neighbour(padded, 0, 0)
    perm_center = neighbour(perm_pad, 0, 0)
    applied = storage_in * center
    for dimension in range(3):
        for offset in (-1, 1):
            transmit = conduct(perm_center, neighbour(perm_pad, dimension, offset))
            applied = applied + transmit * (center - neighbour(padded, dimension, offset))
    return applied


def line_mask(length, low_side, high_side, position, blocks):
    places = jnp.arange(length + 2, dtype=jnp.int32)
    inside = (places >= 1 - low_side) & (places <= length + high_side)
    ingrid = ((places >= 1) | (position > 0)) & ((places <= length) | (position < blocks - 1))
    return (inside & ingrid).astype(jnp.float32)


def local_solve(residual_ext, perm_pad, storage_ext, keep_mask, inverse):
    source = keep_mask * residual_ext
    solved = RELAXATION * inverse * source
    for sweep_count in range(SWEEPS - 1):
        applied = stencil(jnp.pad(solved, 1), perm_pad, storage_ext)
        solved = solved + RELAXATION * inverse * (source - applied)
    return solved[1:-1, 1:-1, 1:-1]


def reference(right_side, permeability, storage, deflation, coarse_inverse, owners, margin):
    perm_pad2 = jnp.pad(permeability, 2)
    perm_pad1 = jnp.pad(permeability, 1)
    storage_pad = jnp.pad(storage, 1)
    vector_blocks = deflation.reshape(NV, N_GZ, CZ, N_GX, CX, N_GY, CY)

    def schwarz_local(residual):
        residual_pad = jnp.pad(residual, 1)

        def one_block(flat_index):
            brick_z = flat_index // (N_GX * N_GY)
            brick_x = (flat_index // N_GY) % N_GX
            brick_y = flat_index % N_GY
            starts = (brick_z * CZ, brick_x * CX, brick_y * CY)
            residual_ext = lax.dynamic_slice(residual_pad, starts, (CZ + 2, CX + 2, CY + 2))
            perm_ext = lax.dynamic_slice(perm_pad2, starts, (CZ + 4, CX + 4, CY + 4))
            storage_ext = lax.dynamic_slice(storage_pad, starts, (CZ + 2, CX + 2, CY + 2))
            depths = margin[brick_z, brick_x, brick_y]
            keep_mask = (line_mask(CZ, depths[0], depths[1], brick_z, N_GZ)[:, None, None]
                         * line_mask(CX, depths[2], depths[3], brick_x, N_GX)[None, :, None]
                         * line_mask(CY, depths[4], depths[5], brick_y, N_GY)[None, None, :])
            diagonal = diagonal_of(perm_ext, storage_ext)
            inverse = keep_mask / jnp.where(keep_mask > 0, diagonal, 1.0)
            return local_solve(residual_ext, perm_ext, storage_ext, keep_mask, inverse)

        pieces = lax.map(one_block, jnp.arange(N_GZ * N_GX * N_GY, dtype=jnp.int32))
        pieces = pieces.reshape(N_GZ, N_GX, N_GY, CZ, CX, CY).transpose(0, 3, 1, 4, 2, 5)
        return pieces.reshape(NZ, NX, NY)

    def coarse_part(residual):
        residual_blocks = residual.reshape(N_GZ, CZ, N_GX, CX, N_GY, CY)
        coefficients = jnp.einsum('kaibjcl,aibjcl->abck', vector_blocks, residual_blocks, precision=PRECISE)
        vector = jnp.zeros((COARSE,), jnp.float32).at[owners.reshape(-1)].set(coefficients.reshape(-1))
        solved = jnp.dot(coarse_inverse, vector, precision=PRECISE)
        picked = solved[owners]
        correction = jnp.einsum('kaibjcl,abck->aibjcl', vector_blocks, picked, precision=PRECISE)
        return correction.reshape(NZ, NX, NY)

    def precondition(residual):
        return schwarz_local(residual) + coarse_part(residual)

    def operate(direction):
        return stencil(jnp.pad(direction, 1), perm_pad1, storage)

    solution = jnp.zeros((NZ, NX, NY), jnp.float32)
    residual = right_side
    precond = precondition(residual)
    direction = precond
    inner_prod = jnp.sum(residual * precond)
    for iteration in range(ITERS):
        applied = operate(direction)
        step_size = inner_prod / jnp.sum(direction * applied)
        solution = solution + step_size * direction
        residual = residual - step_size * applied
        if iteration + 1 < ITERS:
            precond = precondition(residual)
            fresh_prod = jnp.sum(residual * precond)
            direction = precond + (fresh_prod / inner_prod) * direction
            inner_prod = fresh_prod
    return (solution, residual)
```

```python
import jax
import jax.numpy as jnp
from jax import lax
from jax.experimental import pallas as pl
from jax.experimental.pallas import tpu as pltpu
from jax.sharding import PartitionSpec as P

ITERS = 4
RELAX = 0.7
MESH = pl.DeviceIdType.MESH
F32 = jnp.float32
CZ, CX, CY, NV = 8, 64, 128, 8
GROUP = 16
ROUNDS = ITERS + 1
HALOS = 2 + 2 * ITERS


def conduct(a, b):
    return 2.0 * a * b / jnp.maximum(a + b, 0.05)


def fold(plane):
    total = plane[0:8]
    for part in range(1, CX // 8):
        total = total + plane[8 * part : 8 * part + 8]
    return total


def kernel(
    b_ref, perm_ref, sto_ref, w_ref, cinv_ref, own_ref, mar_ref,
    x_ref, r_ref,
    vpad, zpad, p_ref, ap_ref, az_ref, d_ref, s_ref, tz, txl, txh, tyl, tyh,
    hz, hx, hy, sz, sx, sy, vhx, vhy, qpz, qpx, qpy,
    buf_a, buf_b, own_c, pick, rows, gmat, c_ref, cap_ref,
    halo_send, halo_recv, a_send, a_recv, b_send, b_recv, set_send, set_recv,
):
    gx, gy, gz = lax.axis_index("gx"), lax.axis_index("gy"), lax.axis_index("gz")
    ngx, ngy = lax.axis_size("gx"), lax.axis_size("gy")
    me = gy * 2 + gz

    def brick_peer(step):
        other = lax.rem(me + step, GROUP)
        return {"gy": other // 2, "gz": lax.rem(other, 2)}

    def line_peer(step):
        return {"gx": lax.rem(gx + step, GROUP)}

    barrier = pltpu.get_barrier_semaphore()
    for step in range(1, GROUP):
        pl.semaphore_signal(barrier, inc=1, device_id=brick_peer(step), device_id_type=MESH)
        pl.semaphore_signal(barrier, inc=1, device_id=line_peer(step), device_id_type=MESH)

    lane = lax.broadcasted_iota(jnp.int32, (8, 128), 1)
    row = lax.broadcasted_iota(jnp.int32, (8, 128), 0)
    lane_p = lax.broadcasted_iota(jnp.int32, (CX, CY), 1)
    row_p = lax.broadcasted_iota(jnp.int32, (CX, CY), 0)

    def remote(src, dst, send, recv, device):
        return pltpu.make_async_remote_copy(
            src_ref=src, dst_ref=dst, send_sem=send, recv_sem=recv, device_id=device, device_id_type=MESH
        )

    def halo_copies(e):
        left, right = {"gx": lax.rem(gx + ngx - 1, ngx)}, {"gx": lax.rem(gx + 1, ngx)}
        down, up = {"gy": lax.rem(gy + ngy - 1, ngy)}, {"gy": lax.rem(gy + 1, ngy)}
        return [
            remote(sz.at[e], hz.at[e], halo_send.at[e, 0], halo_recv.at[e, 0], {"gz": 1 - gz}),
            remote(sx.at[e, 0], hx.at[e, 1], halo_send.at[e, 1], halo_recv.at[e, 1], left),
            remote(sx.at[e, 1], hx.at[e, 0], halo_send.at[e, 2], halo_recv.at[e, 2], right),
            remote(sy.at[e, 0], hy.at[e, 1], halo_send.at[e, 3], halo_recv.at[e, 3], down),
            remote(sy.at[e, 1], hy.at[e, 0], halo_send.at[e, 4], halo_recv.at[e, 4], up),
        ]

    def halo_start(e):
        for copy in halo_copies(e):
            copy.start()

    def halo_wait(e):
        for copy in halo_copies(e):
            copy.wait_recv()

    def halo_drain(e):
        for copy in halo_copies(e):
            copy.wait_send()

    def pack(e, i, plane, low, high):
        if i == 0:
            sz[e] = plane
        if i == CZ - 1:
            sz[e] = jnp.where(gz == 0, plane, sz[e])
        sx[e, 0, i : i + 1, :] = plane[0:1, :]
        sx[e, 1, i : i + 1, :] = plane[CX - 1 : CX, :]
        for part in range(CX // 8):
            place = 8 * i + part
            piece = plane[8 * part : 8 * part + 8, :]
            low = jnp.where(lane == place, pltpu.roll(piece, place, 1) if place else piece, low)
            high = jnp.where(lane == place, pltpu.roll(piece, place + 1, 1), high)
        if i == CZ - 1:
            sy[e, 0] = low
            sy[e, 1] = high
        return low, high

    def shifted(i, plane, xlow, xhigh, ylow, yhigh):
        parts_low, parts_high = [], []
        for part in range(CX // 8):
            place = 8 * i + part
            parts_low.append(pltpu.roll(ylow, (128 - place) % 128, 1) if place else ylow)
            parts_high.append(pltpu.roll(yhigh, 127 - place, 1))
        x_minus = jnp.where(row_p == 0, xlow[i : i + 1, :], pltpu.roll(plane, 1, 0))
        x_plus = jnp.where(row_p == CX - 1, xhigh[i : i + 1, :], pltpu.roll(plane, CX - 1, 0))
        y_minus = jnp.where(lane_p == 0, jnp.concatenate(parts_low, 0), pltpu.roll(plane, 1, 1))
        y_plus = jnp.where(lane_p == CY - 1, jnp.concatenate(parts_high, 0), pltpu.roll(plane, CY - 1, 1))
        return x_minus, x_plus, y_minus, y_plus

    def neighbours(i, padded, xlow, xhigh, ylow, yhigh):
        x_minus, x_plus, y_minus, y_plus = shifted(i, padded[i + 1], xlow, xhigh, ylow, yhigh)
        total = tz[i] * padded[i] + tz[i + 1] * padded[i + 2]
        total = total + txl[i] * x_minus + txh[i] * x_plus
        return total + tyl[i] * y_minus + tyh[i] * y_plus

    def a_copies(k):
        return [
            remote(buf_a.at[k, me], buf_a.at[k, me], a_send.at[k], a_recv.at[k], brick_peer(step))
            for step in range(1, GROUP)
        ]

    def b_copies(k):
        return [
            remote(buf_b.at[k, gx], buf_b.at[k, gx], b_send.at[k], b_recv.at[k], line_peer(step))
            for step in range(1, GROUP)
        ]

    def a_all(k):
        part = buf_a.at[k, pl.ds(0, GROUP - 1)]
        return remote(part, part, a_send.at[k], a_recv.at[k], brick_peer(1))

    def b_all(k):
        part = buf_b.at[k, pl.ds(0, GROUP - 1)]
        return remote(part, part, b_send.at[k], b_recv.at[k], line_peer(1))

    def coefficient_row(parts):
        stacked = jnp.zeros((8, 128), F32)
        for index in range(NV):
            stacked = jnp.where(row == index, jnp.sum(parts[index], 0, keepdims=True), stacked)
        sums = jnp.sum(stacked, 1, keepdims=True)
        return jnp.sum(jnp.where(lane == 8 * me + row, sums, 0.0), 0, keepdims=True)

    def scalar_row(parts):
        stacked = jnp.zeros((8, 128), F32)
        for index, part in enumerate(parts):
            stacked = jnp.where(row == index, jnp.sum(part, 0, keepdims=True), stacked)
        sums = jnp.sum(stacked, 1, keepdims=True)
        return jnp.sum(jnp.where(lane == row, sums, 0.0), 0, keepdims=True)

    def pass_on(k):
        a_all(k).wait_recv()
        total = buf_a[k, 0]
        for slot in range(1, GROUP):
            total = total + buf_a[k, slot]
        buf_b[k, gx] = total
        for copy in b_copies(k):
            copy.start()
        b_all(k).wait_recv()

    own_rows = jnp.zeros((8, 128), jnp.int32)
    for index in range(NV):
        own_rows = jnp.where(row == index, own_ref[0, 0, 0, index], own_rows)
    own_c[gx] = own_rows
    own_lane = jnp.sum(jnp.where(lane == 8 * me + row, own_rows, 0).astype(F32), 0, keepdims=True)

    zero8 = jnp.zeros((8, 128), F32)
    low, high = zero8, zero8
    for i in range(CZ):
        low, high = pack(0, i, perm_ref[i], low, high)
    pl.semaphore_wait(barrier, 2 * (GROUP - 1))

    for step in range(1, GROUP):
        remote(own_c.at[gx], own_c.at[gx], set_send.at[0], set_recv.at[0], line_peer(step)).start()
    halo_start(0)

    parts = [zero8] * NV
    for i in range(CZ):
        source = b_ref[i]
        for index in range(NV):
            parts[index] = parts[index] + fold(w_ref[index, i] * source)
    buf_a[0, me] = jnp.concatenate([coefficient_row(parts), own_lane], 0)
    for copy in a_copies(0):
        copy.start()

    halo_wait(0)
    in_left = jnp.where(gx > 0, 1.0, 0.0)
    in_right = jnp.where(gx < ngx - 1, 1.0, 0.0)
    in_down = jnp.where(gy > 0, 1.0, 0.0)
    in_up = jnp.where(gy < ngy - 1, 1.0, 0.0)
    in_low = jnp.where(gz > 0, 1.0, 0.0)
    p_xl, p_xh = hx[0, 0] * in_left, hx[0, 1] * in_right
    p_yl, p_yh = hy[0, 0] * in_down, hy[0, 1] * in_up
    tz[0] = conduct(perm_ref[0], hz[0] * in_low)
    tz[CZ] = conduct(perm_ref[CZ - 1], hz[0] * (1.0 - in_low))
    for i in range(1, CZ):
        tz[i] = conduct(perm_ref[i - 1], perm_ref[i])
    vpad[0] = jnp.zeros((CX, CY), F32)
    vpad[CZ + 1] = jnp.zeros((CX, CY), F32)
    zpad[0] = jnp.zeros((CX, CY), F32)
    zpad[CZ + 1] = jnp.zeros((CX, CY), F32)
    low, high = zero8, zero8
    for i in range(CZ):
        center = perm_ref[i]
        x_minus, x_plus, y_minus, y_plus = shifted(i, center, p_xl, p_xh, p_yl, p_yh)
        t_xl, t_xh = conduct(center, x_minus), conduct(center, x_plus)
        t_yl, t_yh = conduct(center, y_minus), conduct(center, y_plus)
        txl[i], txh[i], tyl[i], tyh[i] = t_xl, t_xh, t_yl, t_yh
        diagonal = sto_ref[i] + tz[i] + tz[i + 1] + t_xl + t_xh + t_yl + t_yh
        d_ref[i] = diagonal
        relax = RELAX / diagonal
        s_ref[i] = relax
        source = b_ref[i]
        v = relax * source
        vpad[i + 1] = v
        low, high = pack(1, i, v, low, high)
        r_ref[i] = source
        x_ref[i] = jnp.zeros((CX, CY), F32)
        p_ref[i] = jnp.zeros((CX, CY), F32)
        ap_ref[i] = jnp.zeros((CX, CY), F32)
    halo_start(1)

    owned = own_c.at[pl.ds(0, GROUP - 1)]
    remote(owned, owned, set_send.at[0], set_recv.at[0], line_peer(1)).wait_recv()
    wanted = own_c[...].reshape(GROUP * NV, 128)
    lane_w = lax.broadcasted_iota(jnp.int32, (GROUP * NV, 128), 1)
    picked = jnp.zeros((GROUP * NV, 128), F32)
    for part in range(GROUP):
        one_hot = jnp.where(wanted == lane_w + 128 * part, 1.0, 0.0).astype(F32)
        picked = picked + lax.dot_general(
            one_hot, cinv_ref[:, 128 * part : 128 * part + 128], (((1,), (1,)), ((), ())),
            precision=lax.Precision.HIGHEST, preferred_element_type=F32,
        )
    pick[...] = picked.reshape(GROUP, NV, 128)
    for step in range(1, GROUP):
        other = lax.rem(gx + step, GROUP)
        remote(pick.at[other], rows.at[gx], set_send.at[1], set_recv.at[1], {"gx": other}).start()
    rows[gx] = pick[gx]

    pass_on(0)
    c_ref[...] = buf_b[0, :, 0, :]
    cap_ref[...] = jnp.zeros((GROUP, 128), F32)
    got = rows.at[pl.ds(0, GROUP - 1)]
    remote(got, got, set_send.at[1], set_recv.at[1], line_peer(1)).wait_recv()
    order = buf_b[0, :, 1, :].astype(jnp.int32)
    for part in range(GROUP):
        index = jnp.broadcast_to(order[part : part + 1, :], (8, 128))
        inside, block = index & 127, index >> 7
        chosen = zero8
        for source_part in range(GROUP):
            moved = jnp.take_along_axis(rows[source_part], inside, axis=1)
            chosen = jnp.where(block == source_part, moved, chosen)
        gmat[part] = chosen

    keep = [mar_ref[0, 0, 0, side].astype(F32) for side in range(6)]
    keep_z = jnp.where(gz > 0, keep[0], keep[1])
    halo_plane = (CZ + 1) * (1 - gz)
    halo_wait(1)
    vpad[halo_plane] = hz[1] * keep_z
    vhx[0], vhx[1] = hx[1, 0] * keep[2], hx[1, 1] * keep[3]
    vhy[0], vhy[1] = hy[1, 0] * keep[4], hy[1, 1] * keep[5]
    qpz[...] = jnp.zeros((CX, CY), F32)
    for side in range(2):
        qpx[side], qpy[side] = zero8, zero8

    def iteration(k, carry):
        rz_old, pap_old = carry
        e_z, e_q = 2 + 2 * k, 3 + 2 * k
        total = zero8
        for part in range(GROUP):
            total = total + gmat[part] * c_ref[part : part + 1, :]
        y_rows = jnp.broadcast_to(jnp.sum(total, 1, keepdims=True), (8, 128))
        xl, xh, yl, yh = vhx[0], vhx[1], vhy[0], vhy[1]
        low, high, rz_part = zero8, zero8, zero8
        for i in range(CZ):
            z = 1.3 * vpad[i + 1] + s_ref[i] * neighbours(i, vpad, xl, xh, yl, yh)
            for index in range(NV):
                z = z + w_ref[index, i] * y_rows[index : index + 1, :]
            zpad[i + 1] = z
            rz_part = rz_part + fold(r_ref[i] * z)
            low, high = pack(e_z, i, z, low, high)
        halo_start(e_z)
        halo_wait(e_z)
        zpad[halo_plane] = hz[e_z]
        xl, xh, yl, yh = hx[e_z, 0], hx[e_z, 1], hy[e_z, 0], hy[e_z, 1]
        low, high, zaz_part, zap_part = zero8, zero8, zero8, zero8
        parts = [zero8] * NV
        for i in range(CZ):
            z = zpad[i + 1]
            az = d_ref[i] * z - neighbours(i, zpad, xl, xh, yl, yh)
            az_ref[i] = az
            zaz_part = zaz_part + fold(z * az)
            zap_part = zap_part + fold(z * ap_ref[i])
            for index in range(NV):
                parts[index] = parts[index] + fold(w_ref[index, i] * az)
            low, high = pack(e_q, i, s_ref[i] * az, low, high)
        slot = k + 1
        buf_a[slot, me] = jnp.concatenate(
            [coefficient_row(parts), scalar_row([rz_part, zaz_part, zap_part])], 0
        )
        for copy in a_copies(slot):
            copy.start()
        halo_start(e_q)
        pass_on(slot)
        scalars = jnp.sum(buf_b[slot, :, 1, :], 0, keepdims=True)
        rz, zaz, zap = scalars[:, 0:1], scalars[:, 1:2], scalars[:, 2:3]
        beta = jnp.where(k == 0, 0.0, rz / rz_old)
        pap = zaz + beta * (2.0 * zap + beta * pap_old)
        alpha = rz / pap
        for i in range(CZ):
            p = zpad[i + 1] + beta * p_ref[i]
            ap = az_ref[i] + beta * ap_ref[i]
            p_ref[i], ap_ref[i] = p, ap
            x_ref[i] = x_ref[i] + alpha * p
            r = r_ref[i] - alpha * ap
            r_ref[i] = r
            vpad[i + 1] = s_ref[i] * r
        cap = buf_b[slot, :, 0, :] + beta * cap_ref[...]
        cap_ref[...] = cap
        c_ref[...] = c_ref[...] - alpha * cap
        halo_wait(e_q)
        fresh = hz[e_q] + beta * qpz[...]
        qpz[...] = fresh
        vpad[halo_plane] = vpad[halo_plane] - (alpha * keep_z) * fresh
        for side in range(2):
            fresh = hx[e_q, side] + beta * qpx[side]
            qpx[side] = fresh
            vhx[side] = vhx[side] - (alpha * keep[2 + side]) * fresh
            fresh = hy[e_q, side] + beta * qpy[side]
            qpy[side] = fresh
            vhy[side] = vhy[side] - (alpha * keep[4 + side]) * fresh
        return rz, pap

    one = jnp.ones((1, 1), F32)
    lax.fori_loop(0, ITERS, iteration, (one, jnp.zeros((1, 1), F32)))

    for e in range(HALOS):
        halo_drain(e)
    for k in range(ROUNDS):
        a_all(k).wait_send()
        b_all(k).wait_send()
    remote(owned, owned, set_send.at[0], set_recv.at[0], line_peer(1)).wait_send()
    remote(got, got, set_send.at[1], set_recv.at[1], line_peer(1)).wait_send()


def local(right_side, permeability, storage, deflation, coarse_inverse, owners, margin):
    vmem = pl.BlockSpec(memory_space=pltpu.VMEM)
    smem = pl.BlockSpec(memory_space=pltpu.SMEM)
    field = pltpu.VMEM((CZ, CX, CY), F32)
    shape = jax.ShapeDtypeStruct((CZ, CX, CY), F32)
    dma = pltpu.SemaphoreType.DMA
    return pl.pallas_call(
        kernel,
        out_shape=(shape, shape),
        in_specs=[vmem] * 5 + [smem] * 2,
        out_specs=(vmem, vmem),
        scratch_shapes=[
            pltpu.VMEM((CZ + 2, CX, CY), F32),
            pltpu.VMEM((CZ + 2, CX, CY), F32),
            field, field, field, field, field,
            pltpu.VMEM((CZ + 1, CX, CY), F32),
            field, field, field, field,
            pltpu.VMEM((HALOS, CX, CY), F32),
            pltpu.VMEM((HALOS, 2, 8, 128), F32),
            pltpu.VMEM((HALOS, 2, 8, 128), F32),
            pltpu.VMEM((HALOS, CX, CY), F32),
            pltpu.VMEM((HALOS, 2, 8, 128), F32),
            pltpu.VMEM((HALOS, 2, 8, 128), F32),
            pltpu.VMEM((2, 8, 128), F32),
            pltpu.VMEM((2, 8, 128), F32),
            pltpu.VMEM((CX, CY), F32),
            pltpu.VMEM((2, 8, 128), F32),
            pltpu.VMEM((2, 8, 128), F32),
            pltpu.VMEM((ROUNDS, GROUP, 2, 128), F32),
            pltpu.VMEM((ROUNDS, GROUP, 2, 128), F32),
            pltpu.VMEM((GROUP, 8, 128), jnp.int32),
            pltpu.VMEM((GROUP, 8, 128), F32),
            pltpu.VMEM((GROUP, 8, 128), F32),
            pltpu.VMEM((GROUP, 8, 128), F32),
            pltpu.VMEM((GROUP, 128), F32),
            pltpu.VMEM((GROUP, 128), F32),
            dma((HALOS, 5)), dma((HALOS, 5)),
            dma((ROUNDS,)), dma((ROUNDS,)), dma((ROUNDS,)), dma((ROUNDS,)),
            dma((2,)), dma((2,)),
        ],
        compiler_params=pltpu.CompilerParams(
            collective_id=0, has_side_effects=True, vmem_limit_bytes=40 * 1024 * 1024
        ),
    )(right_side, permeability, storage, deflation, coarse_inverse, owners, margin)


def solution(mesh):
    in_specs = (
        P("gz", "gx", "gy"),
        P("gz", "gx", "gy"),
        P("gz", "gx", "gy"),
        P(None, "gz", "gx", "gy"),
        P("gx", None),
        P("gz", "gx", "gy", None),
        P("gz", "gx", "gy", None),
    )
    out_specs = (P("gz", "gx", "gy"), P("gz", "gx", "gy"))
    return jax.shard_map(local, mesh=mesh, in_specs=in_specs, out_specs=out_specs, check_vma=False)
```

```python
import jax
import jax.numpy as jnp
from jax import lax
from jax.experimental import pallas as pl
from jax.experimental.pallas import tpu as pltpu
from jax.sharding import PartitionSpec as P

ITERS = 4
RELAX = 0.7
MESH = pl.DeviceIdType.MESH
F32 = jnp.float32
CZ, CX, CY, NV = 8, 64, 128, 8
GROUP = 16
CHIPS = 128
E_PERM, E_V, E_LV, E_Z, E_LOOP = 0, 1, 2, 3, 4
HALOS = E_LOOP + 2 * (ITERS - 1)
LAYER = sorted(
    [(a, b) for a in range(4) for b in range(4)], key=lambda t: -(min(t[0], 4 - t[0]) + min(t[1], 4 - t[1]))
)


def conduct(a, b):
    return 2.0 * a * b / jnp.maximum(a + b, 0.05)


def fold(plane):
    total = plane[0:8]
    for part in range(1, CX // 8):
        total = total + plane[8 * part : 8 * part + 8]
    return total


def kernel(
    b_in, perm_in, sto_in, w_in, cinv_in, own_in, mar_in,
    x_ref, r_ref,
    perm_ref, sto_ref, w_ref, cinv_ref, own_ref, mar_ref,
    qpad, zpad, p_ref, ap_ref, az_ref, d_ref, s_ref, tz, txl, txh, tyl, tyh, lv, lq, lqp,
    hz, hx, hy, sz, sx, sy, qx, qy, zx, zy, lvz, lvx, lvy, lqpz, lqpx, lqpy,
    wz, wx, wy, wxs, wys,
    buf_a, buf_b, pair, wide, own_c, pick, rows, rows_nb, gmat, c_ref, cap_ref,
    in_sem, halo_send, halo_recv, a_send, a_recv, b_send, b_recv, set_send, set_recv,
    w_send, w_recv, g_send, g_recv, pair_send, pair_recv, wide_send, wide_recv,
):
    gx, gy, gz = lax.axis_index("gx"), lax.axis_index("gy"), lax.axis_index("gz")
    ngx, ngy = lax.axis_size("gx"), lax.axis_size("gy")
    me = gy * 2 + gz
    loads = [
        pltpu.make_async_copy(src, dst, in_sem.at[index])
        for index, (src, dst) in enumerate(
            [
                (own_in, own_ref), (perm_in, perm_ref), (b_in, r_ref), (w_in, w_ref),
                (cinv_in, cinv_ref), (sto_in, sto_ref), (mar_in, mar_ref),
            ]
        )
    ]
    for load in loads:
        load.start()

    def brick_peer(step):
        other = lax.rem(me + step, GROUP)
        return {"gy": other // 2, "gz": lax.rem(other, 2)}

    def line_peer(step):
        return {"gx": lax.rem(gx + step, GROUP)}

    barrier = pltpu.get_barrier_semaphore()
    for step in range(1, GROUP):
        pl.semaphore_signal(barrier, inc=1, device_id=brick_peer(step), device_id_type=MESH)
        pl.semaphore_signal(barrier, inc=1, device_id=line_peer(step), device_id_type=MESH)

    lane = lax.broadcasted_iota(jnp.int32, (8, 128), 1)
    row = lax.broadcasted_iota(jnp.int32, (8, 128), 0)
    lane_p = lax.broadcasted_iota(jnp.int32, (CX, CY), 1)
    row_p = lax.broadcasted_iota(jnp.int32, (CX, CY), 0)
    zero8 = jnp.zeros((8, 128), F32)
    zero_p = jnp.zeros((CX, CY), F32)
    partner = {"gz": 1 - gz}
    left, right = {"gx": lax.rem(gx + ngx - 1, ngx)}, {"gx": lax.rem(gx + 1, ngx)}
    down, up = {"gy": lax.rem(gy + ngy - 1, ngy)}, {"gy": lax.rem(gy + 1, ngy)}

    def remote(src, dst, send, recv, device):
        return pltpu.make_async_remote_copy(
            src_ref=src, dst_ref=dst, send_sem=send, recv_sem=recv, device_id=device, device_id_type=MESH
        )

    def halo_copies(e):
        return [
            remote(sz.at[e], hz.at[e], halo_send.at[e, 0], halo_recv.at[e, 0], partner),
            remote(sx.at[e, 0], hx.at[e, 1], halo_send.at[e, 1], halo_recv.at[e, 1], left),
            remote(sx.at[e, 1], hx.at[e, 0], halo_send.at[e, 2], halo_recv.at[e, 2], right),
            remote(sy.at[e, 0], hy.at[e, 1], halo_send.at[e, 3], halo_recv.at[e, 3], down),
            remote(sy.at[e, 1], hy.at[e, 0], halo_send.at[e, 4], halo_recv.at[e, 4], up),
        ]

    def start_all(copies):
        for copy in copies:
            copy.start()

    def recv_all(copies):
        for copy in copies:
            copy.wait_recv()

    def send_all(copies):
        for copy in copies:
            copy.wait_send()

    def columns(i, plane, low, high):
        for part in range(CX // 8):
            place = 8 * i + part
            piece = plane[8 * part : 8 * part + 8, :]
            low = jnp.where(lane == place, pltpu.roll(piece, place, 1) if place else piece, low)
            high = jnp.where(lane == place, pltpu.roll(piece, place + 1, 1), high)
        return low, high

    def pack(e, i, plane, low, high):
        if i == 0:
            sz[e] = plane
        if i == CZ - 1:
            sz[e] = jnp.where(gz == 0, plane, sz[e])
        sx[e, 0, i : i + 1, :] = plane[0:1, :]
        sx[e, 1, i : i + 1, :] = plane[CX - 1 : CX, :]
        low, high = columns(i, plane, low, high)
        if i == CZ - 1:
            sy[e, 0] = low
            sy[e, 1] = high
        return low, high

    def shifted(i, plane, xlow, xhigh, ylow, yhigh):
        parts_low, parts_high = [], []
        for part in range(CX // 8):
            place = 8 * i + part
            parts_low.append(pltpu.roll(ylow, (128 - place) % 128, 1) if place else ylow)
            parts_high.append(pltpu.roll(yhigh, 127 - place, 1))
        x_minus = jnp.where(row_p == 0, xlow[i : i + 1, :], pltpu.roll(plane, 1, 0))
        x_plus = jnp.where(row_p == CX - 1, xhigh[i : i + 1, :], pltpu.roll(plane, CX - 1, 0))
        y_minus = jnp.where(lane_p == 0, jnp.concatenate(parts_low, 0), pltpu.roll(plane, 1, 1))
        y_plus = jnp.where(lane_p == CY - 1, jnp.concatenate(parts_high, 0), pltpu.roll(plane, CY - 1, 1))
        return x_minus, x_plus, y_minus, y_plus

    def neighbours(i, padded, xlow, xhigh, ylow, yhigh):
        x_minus, x_plus, y_minus, y_plus = shifted(i, padded[i + 1], xlow, xhigh, ylow, yhigh)
        total = tz[i] * padded[i] + tz[i + 1] * padded[i + 2]
        total = total + txl[i] * x_minus + txh[i] * x_plus
        return total + tyl[i] * y_minus + tyh[i] * y_plus

    def a_copies():
        return [remote(buf_a.at[me], buf_a.at[me], a_send, a_recv, brick_peer(step)) for step in range(1, GROUP)]

    def b_copies():
        return [remote(buf_b.at[gx], buf_b.at[gx], b_send, b_recv, line_peer(step)) for step in range(1, GROUP)]

    a_part, b_part = buf_a.at[pl.ds(0, GROUP - 1)], buf_b.at[pl.ds(0, GROUP - 1)]
    a_all = remote(a_part, a_part, a_send, a_recv, brick_peer(1))
    b_all = remote(b_part, b_part, b_send, b_recv, line_peer(1))

    chip = gy * GROUP + gx
    cx, cy = lax.rem(gx, 4), gx // 4

    def pair_copy(k):
        return remote(pair.at[k, gz], pair.at[k, gz], pair_send.at[k], pair_recv.at[k], partner)

    def wide_start(k):
        line = wide.at[k, pl.ds(chip, 1), :]

        def send(dz, dy, dx):
            device = {"gx": lax.rem(cy + dy, 4) * 4 + lax.rem(cx + dx, 4), "gy": lax.rem(gy + dz, ngy)}
            remote(line, line, wide_send.at[k], wide_recv.at[k], device).start()

        def layer(j, carry):
            off = (j + 1) // 2
            dz = jnp.where(lax.rem(j, 2) == 1, 4 - off, 4 + off)
            for dy, dx in LAYER:
                send(dz, dy, dx)
            return carry

        lax.fori_loop(0, 7, layer, 0)
        for dy, dx in LAYER[:-1]:
            send(0, dy, dx)

    def wide_all(k):
        part = wide.at[k, pl.ds(0, CHIPS - 1), :]
        return remote(part, part, wide_send.at[k], wide_recv.at[k], right)

    def lane_sums(parts):
        stacked = zero8
        for index, part in enumerate(parts):
            stacked = jnp.where(row == index, jnp.sum(part, 0, keepdims=True), stacked)
        return jnp.sum(stacked, 1, keepdims=True)

    def coefficient_row(parts):
        return jnp.sum(jnp.where(lane == 8 * me + row, lane_sums(parts), 0.0), 0, keepdims=True)

    def scalar_row(parts):
        place = GROUP * lax.rem(gy + 1, ngy)
        return jnp.sum(jnp.where(lane == place + row, lane_sums(parts), 0.0), 0, keepdims=True)

    def exchange(k, message, middle):
        pair[k, gz] = message
        pair_copy(k).start()
        middle()
        pair_copy(k).wait_recv()
        wide[k, pl.ds(chip, 1), :] = pair[k, 0] + pair[k, 1]
        wide_start(k)

    def exchanged(k):
        wide_all(k).wait_recv()
        block = lax.broadcasted_iota(jnp.int32, (GROUP, 128), 1) // GROUP
        coefficients, scalars = jnp.zeros((GROUP, 128), F32), jnp.zeros((GROUP, 128), F32)
        for index in range(CHIPS // GROUP):
            part = wide[k, GROUP * index : GROUP * index + GROUP, :]
            coefficients = jnp.where(block == index, part, coefficients)
            scalars = jnp.where(block == (index + 1) % (CHIPS // GROUP), part, scalars)
        line = jnp.sum(scalars, 0, keepdims=True)
        spot = lax.rem(lane[0:1, :], GROUP)
        sums = [jnp.sum(jnp.where(spot == index, line, 0.0), 1, keepdims=True) for index in range(3)]
        return coefficients, sums

    loads[0].wait()
    own_line = jnp.concatenate([own_ref[0, 0], jnp.zeros((1, 120), jnp.int32)], 1)
    own_rows = jnp.sum(jnp.where(lane == row, own_line, 0).astype(F32), 1, keepdims=True)
    own_c[gx] = jnp.broadcast_to(own_rows, (8, 128))
    own_lane = jnp.sum(jnp.where(lane == 8 * me + row, own_rows, 0.0), 0, keepdims=True)

    loads[1].wait()
    low, high = zero8, zero8
    for i in range(CZ):
        low, high = pack(E_PERM, i, perm_ref[i], low, high)
    pl.semaphore_wait(barrier, 2 * (GROUP - 1))

    for step in range(1, GROUP):
        remote(own_c.at[gx], own_c.at[gx], set_send.at[0], set_recv.at[0], line_peer(step)).start()
    start_all(halo_copies(E_PERM))

    loads[2].wait()
    loads[3].wait()
    parts = [zero8] * NV
    for i in range(CZ):
        source = r_ref[i]
        for index in range(NV):
            parts[index] = parts[index] + fold(w_ref[index, i] * source)
    buf_a[me] = jnp.concatenate([coefficient_row(parts), own_lane], 0)
    start_all(a_copies())

    loads[5].wait()
    loads[6].wait()
    recv_all(halo_copies(E_PERM))
    in_left = jnp.where(gx > 0, 1.0, 0.0)
    in_right = jnp.where(gx < ngx - 1, 1.0, 0.0)
    in_down = jnp.where(gy > 0, 1.0, 0.0)
    in_up = jnp.where(gy < ngy - 1, 1.0, 0.0)
    in_low = jnp.where(gz > 0, 1.0, 0.0)
    p_xl, p_xh = hx[E_PERM, 0] * in_left, hx[E_PERM, 1] * in_right
    p_yl, p_yh = hy[E_PERM, 0] * in_down, hy[E_PERM, 1] * in_up
    tz[0] = conduct(perm_ref[0], hz[E_PERM] * in_low)
    tz[CZ] = conduct(perm_ref[CZ - 1], hz[E_PERM] * (1.0 - in_low))
    for i in range(1, CZ):
        tz[i] = conduct(perm_ref[i - 1], perm_ref[i])
    for plane in (0, CZ + 1):
        qpad[plane] = zero_p
        zpad[plane] = zero_p
    low, high = zero8, zero8
    for i in range(CZ):
        center = perm_ref[i]
        x_minus, x_plus, y_minus, y_plus = shifted(i, center, p_xl, p_xh, p_yl, p_yh)
        t_xl, t_xh = conduct(center, x_minus), conduct(center, x_plus)
        t_yl, t_yh = conduct(center, y_minus), conduct(center, y_plus)
        txl[i], txh[i], tyl[i], tyh[i] = t_xl, t_xh, t_yl, t_yh
        diagonal = sto_ref[i] + tz[i] + tz[i + 1] + t_xl + t_xh + t_yl + t_yh
        d_ref[i] = diagonal
        relax = RELAX / diagonal
        s_ref[i] = relax
        v = relax * r_ref[i]
        qpad[i + 1] = v
        low, high = pack(E_V, i, v, low, high)
    start_all(halo_copies(E_V))

    loads[4].wait()
    owned = own_c.at[pl.ds(0, GROUP - 1)]
    own_all = remote(owned, owned, set_send.at[0], set_recv.at[0], right)
    own_all.wait_recv()
    wanted = own_c[...].reshape(GROUP * NV, 128).astype(jnp.int32)
    lane_w = lax.broadcasted_iota(jnp.int32, (GROUP * NV, 128), 1)
    one_hot = jnp.concatenate(
        [jnp.where(wanted == lane_w + 128 * part, 1.0, 0.0).astype(F32) for part in range(GROUP)], 1
    )
    picked = lax.dot_general(
        one_hot, cinv_ref[...], (((1,), (1,)), ((), ())),
        precision=lax.Precision.HIGHEST, preferred_element_type=F32,
    )
    pick[...] = picked.reshape(GROUP, NV, 128)
    for step in range(1, GROUP):
        other = lax.rem(gx + step, GROUP)
        remote(pick.at[other], rows.at[gx], set_send.at[1], set_recv.at[1], {"gx": other}).start()
    rows[gx] = pick[gx]

    a_all.wait_recv()
    total = buf_a[0]
    for slot in range(1, GROUP):
        total = total + buf_a[slot]
    buf_b[gx] = total
    start_all(b_copies())

    keep = [mar_ref[0, 0, 0:1, side : side + 1].astype(F32) for side in range(6)]
    keep_z = jnp.where(gz > 0, keep[0], keep[1])
    halo_plane = (CZ + 1) * (1 - gz)

    def local_pass(e, out, e_out):
        recv_all(halo_copies(e))
        qpad[halo_plane] = hz[e] * keep_z
        q_xl, q_xh = hx[e, 0] * keep[2], hx[e, 1] * keep[3]
        q_yl, q_yh = hy[e, 0] * keep[4], hy[e, 1] * keep[5]
        low, high = zero8, zero8
        for i in range(CZ):
            value = 1.3 * qpad[i + 1] + s_ref[i] * neighbours(i, qpad, q_xl, q_xh, q_yl, q_yh)
            out[i] = value
            low, high = pack(e_out, i, value, low, high)
        start_all(halo_copies(e_out))

    local_pass(E_V, lv, E_LV)

    for index in range(NV):
        low, high = zero8, zero8
        for i in range(CZ):
            plane = w_ref[index, i]
            wxs[0, index, i : i + 1, :] = plane[0:1, :]
            wxs[1, index, i : i + 1, :] = plane[CX - 1 : CX, :]
            low, high = columns(i, plane, low, high)
        wys[0, index] = low
        wys[1, index] = high
    w_copies = [
        remote(w_ref.at[:, (CZ - 1) * (1 - gz)], wz, w_send.at[0], w_recv.at[0], partner),
        remote(wxs.at[0], wx.at[1], w_send.at[1], w_recv.at[1], left),
        remote(wxs.at[1], wx.at[0], w_send.at[2], w_recv.at[2], right),
        remote(wys.at[0], wy.at[1], w_send.at[3], w_recv.at[3], down),
        remote(wys.at[1], wy.at[0], w_send.at[4], w_recv.at[4], up),
    ]
    start_all(w_copies)

    for i in range(CZ):
        x_ref[i] = zero_p
        p_ref[i] = zero_p
        ap_ref[i] = zero_p
        lqp[i] = zero_p
    lqpz[...] = zero_p
    for side in range(2):
        lqpx[side], lqpy[side] = zero8, zero8
    cap_ref[...] = jnp.zeros((GROUP, 128), F32)

    got = rows.at[pl.ds(0, GROUP - 1)]
    rows_all = remote(got, got, set_send.at[1], set_recv.at[1], right)
    rows_all.wait_recv()
    g_copies = [
        remote(rows, rows_nb.at[place], g_send.at[place], g_recv.at[place], device)
        for place, device in ((0, partner), (2, left), (1, right), (4, down), (3, up))
    ]
    start_all(g_copies)

    b_all.wait_recv()
    c_ref[...] = buf_b[:, 0, :]

    def in_order(source, target):
        order = buf_b[:, 1, :].astype(jnp.int32)
        for part in range(GROUP):
            index = jnp.broadcast_to(order[part : part + 1, :], (8, 128))
            inside, block = index & 127, index >> 7
            chosen = zero8
            for source_part in range(GROUP):
                moved = jnp.take_along_axis(source[source_part], inside, axis=1)
                chosen = jnp.where(block == source_part, moved, chosen)
            target[part] = chosen

    def coarse_solution(matrix):
        total = zero8
        for part in range(GROUP):
            total = total + matrix[part] * c_ref[part : part + 1, :]
        return jnp.broadcast_to(jnp.sum(total, 1, keepdims=True), (8, 128))

    in_order(rows, gmat.at[0])
    y_own = coarse_solution(gmat.at[0])
    low, high, rz_first = zero8, zero8, zero8
    for i in range(CZ):
        z = lv[i]
        for index in range(NV):
            z = z + w_ref[index, i] * y_own[index : index + 1, :]
        zpad[i + 1] = z
        rz_first = rz_first + fold(r_ref[i] * z)
        low, high = pack(E_Z, i, z, low, high)
    start_all(halo_copies(E_Z))
    recv_all(halo_copies(E_LV))
    lvz[...] = hz[E_LV]
    for side in range(2):
        lvx[side], lvy[side] = hx[E_LV, side], hy[E_LV, side]
    recv_all(halo_copies(E_Z))
    zpad[halo_plane] = hz[E_Z]
    for side in range(2):
        zx[side], zy[side] = hx[E_Z, side], hy[E_Z, side]

    def image_pass(last):
        xl, xh, yl, yh = zx[0], zx[1], zy[0], zy[1]
        zaz, zap = zero8, zero8
        parts = [zero8] * NV
        for i in range(CZ):
            z = zpad[i + 1]
            az = d_ref[i] * z - neighbours(i, zpad, xl, xh, yl, yh)
            az_ref[i] = az
            zaz = zaz + fold(z * az)
            zap = zap + fold(z * ap_ref[i])
            if not last:
                for index in range(NV):
                    parts[index] = parts[index] + fold(w_ref[index, i] * az)
        return zaz, zap, parts

    def steps(rz, zaz, zap, rz_old, pap_old, first):
        beta = jnp.where(first, 0.0, rz / rz_old)
        pap = zaz + beta * (2.0 * zap + beta * pap_old)
        return beta, pap, rz / pap

    def iteration(k, carry):
        rz_part, rz_old, pap_old = carry
        e_q, e_l = E_LOOP + 2 * k, E_LOOP + 1 + 2 * k
        zaz, zap, parts = image_pass(False)
        message = coefficient_row(parts) + scalar_row([rz_part, zaz, zap])

        def send_q():
            low, high = zero8, zero8
            for i in range(CZ):
                q = s_ref[i] * az_ref[i]
                qpad[i + 1] = q
                low, high = pack(e_q, i, q, low, high)
            start_all(halo_copies(e_q))

        exchange(k, message, send_q)
        local_pass(e_q, lq, e_l)

        @pl.when(k == 0)
        def _():
            recv_all(w_copies)
            recv_all(g_copies)
            for place in range(5):
                in_order(rows_nb.at[place], gmat.at[place + 1])

        recv_all(halo_copies(e_l))
        fresh_c, sums = exchanged(k)
        rz, zaz, zap = sums
        beta, pap, alpha = steps(rz, zaz, zap, rz_old, pap_old, k == 0)
        cap = fresh_c + beta * cap_ref[...]
        cap_ref[...] = cap
        c_ref[...] = c_ref[...] - alpha * cap
        y_own = coarse_solution(gmat.at[0])
        rz_part = zero8
        for i in range(CZ):
            p = zpad[i + 1] + beta * p_ref[i]
            ap = az_ref[i] + beta * ap_ref[i]
            p_ref[i], ap_ref[i] = p, ap
            x_ref[i] = x_ref[i] + alpha * p
            r = r_ref[i] - alpha * ap
            r_ref[i] = r
            lqd = lq[i] + beta * lqp[i]
            lqp[i] = lqd
            z = lv[i] - alpha * lqd
            lv[i] = z
            for index in range(NV):
                z = z + w_ref[index, i] * y_own[index : index + 1, :]
            zpad[i + 1] = z
            rz_part = rz_part + fold(r * z)
        y_nb = coarse_solution(gmat.at[1])
        lqd = hz[e_l] + beta * lqpz[...]
        lqpz[...] = lqd
        z = lvz[...] - alpha * lqd
        lvz[...] = z
        for index in range(NV):
            z = z + wz[index] * y_nb[index : index + 1, :]
        zpad[halo_plane] = z
        for halo, old, base, vectors, target, first_place in (
            (hx, lqpx, lvx, wx, zx, 2), (hy, lqpy, lvy, wy, zy, 4),
        ):
            for side in range(2):
                y_nb = coarse_solution(gmat.at[first_place + side])
                lqd = halo[e_l, side] + beta * old[side]
                old[side] = lqd
                z = base[side] - alpha * lqd
                base[side] = z
                for index in range(NV):
                    z = z + vectors[side, index] * y_nb[index : index + 1, :]
                target[side] = z
        return rz_part, rz, pap

    one = jnp.ones((1, 1), F32)
    rz_part, rz_old, pap_old = lax.fori_loop(0, ITERS - 1, iteration, (rz_first, one, one))
    zaz, zap, _ = image_pass(True)
    exchange(ITERS - 1, scalar_row([rz_part, zaz, zap]), lambda: None)
    _, sums = exchanged(ITERS - 1)
    beta, pap, alpha = steps(*sums, rz_old, pap_old, False)
    for i in range(CZ):
        x_ref[i] = x_ref[i] + alpha * (zpad[i + 1] + beta * p_ref[i])
        r_ref[i] = r_ref[i] - alpha * (az_ref[i] + beta * ap_ref[i])

    for e in range(HALOS):
        send_all(halo_copies(e))
    for k in range(ITERS):
        pair_copy(k).wait_send()
        wide_all(k).wait_send()
    send_all([a_all, b_all, own_all, rows_all] + w_copies + g_copies)


def local(right_side, permeability, storage, deflation, coarse_inverse, owners, margin):
    hbm = pl.BlockSpec(memory_space=pltpu.HBM)
    vmem = pl.BlockSpec(memory_space=pltpu.VMEM)
    shape = jax.ShapeDtypeStruct((CZ, CX, CY), F32)
    dma = pltpu.SemaphoreType.DMA

    def ram(*dims, dtype=F32):
        return pltpu.VMEM(dims, dtype)

    field, padded = ram(CZ, CX, CY), ram(CZ + 2, CX, CY)
    plane, ends = ram(CX, CY), ram(2, 8, 128)
    return pl.pallas_call(
        kernel,
        out_shape=(shape, shape),
        in_specs=[hbm] * 7,
        out_specs=(vmem, vmem),
        scratch_shapes=[
            field, field, ram(NV, CZ, CX, CY), ram(*coarse_inverse.shape),
            ram(*owners.shape, dtype=jnp.int32), ram(*margin.shape, dtype=jnp.int32),
            padded, padded, field, field, field, field, field, ram(CZ + 1, CX, CY),
            field, field, field, field, field, field, field,
            ram(HALOS, CX, CY), ram(HALOS, 2, 8, 128), ram(HALOS, 2, 8, 128),
            ram(HALOS, CX, CY), ram(HALOS, 2, 8, 128), ram(HALOS, 2, 8, 128),
            ends, ends, ends, ends, plane, ends, ends, plane, ends, ends,
            ram(NV, CX, CY), ram(2, NV, 8, 128), ram(2, NV, 8, 128), ram(2, NV, 8, 128), ram(2, NV, 8, 128),
            ram(GROUP, 2, 128), ram(GROUP, 2, 128), ram(ITERS, 2, 1, 128), ram(ITERS, CHIPS, 128),
            ram(GROUP, 8, 128), ram(GROUP, 8, 128), ram(GROUP, 8, 128), ram(5, GROUP, 8, 128),
            ram(6, GROUP, 8, 128), ram(GROUP, 128), ram(GROUP, 128),
            dma((7,)), dma((HALOS, 5)), dma((HALOS, 5)), dma, dma, dma, dma, dma((2,)), dma((2,)),
            dma((5,)), dma((5,)), dma((5,)), dma((5,)),
            dma((ITERS,)), dma((ITERS,)), dma((ITERS,)), dma((ITERS,)),
        ],
        compiler_params=pltpu.CompilerParams(
            collective_id=0, has_side_effects=True, vmem_limit_bytes=40 * 1024 * 1024
        ),
    )(right_side, permeability, storage, deflation, coarse_inverse, owners, margin)


def solution(mesh):
    in_specs = (
        P("gz", "gx", "gy"),
        P("gz", "gx", "gy"),
        P("gz", "gx", "gy"),
        P(None, "gz", "gx", "gy"),
        P("gx", None),
        P("gz", "gx", "gy", None),
        P("gz", "gx", "gy", None),
    )
    out_specs = (P("gz", "gx", "gy"), P("gz", "gx", "gy"))
    return jax.shard_map(local, mesh=mesh, in_specs=in_specs, out_specs=out_specs, check_vma=False)
```

```python
import jax
import jax.numpy as jnp
from jax import lax
from jax.experimental import pallas as pl
from jax.experimental.pallas import tpu as pltpu
from jax.sharding import PartitionSpec as P

ITERS = 4
RELAX = 0.7
MESH = pl.DeviceIdType.MESH
F32 = jnp.float32
CZ, CX, CY, NV = 8, 64, 128, 8
GROUP = 16
CHIPS = 128
E_PERM, E_V, E_LV, E_LOOP = 0, 1, 2, 3
HALOS = E_LOOP + 2 * (ITERS - 1)
LAYER = sorted(
    [(a, b) for a in range(4) for b in range(4)], key=lambda t: -(min(t[0], 4 - t[0]) + min(t[1], 4 - t[1]))
)

FAR = [(4, dy, dx) for dy, dx in LAYER[:5]] + [(dz, 2, 2) for dz in (3, 5)]


def conduct(a, b):
    return 2.0 * a * b / jnp.maximum(a + b, 0.05)


def fold(plane):
    total = plane[0:8]
    for part in range(1, CX // 8):
        total = total + plane[8 * part : 8 * part + 8]
    return total


def kernel(
    b_in, perm_in, sto_in, w_in, cinv_in, own_in, mar_in,
    x_ref, r_ref,
    perm_ref, sto_ref, w_ref, cinv_ref, own_ref, mar_ref,
    qpad, zpad, p_ref, ap_ref, az_ref, d_ref, s_ref, tz, txl, txh, tyl, tyh, lv, lq, lqp,
    hz, hx, hy, sz, sx, sy, qx, qy, zx, zy, lvz, lvx, lvy, lqpz, lqpx, lqpy,
    wz, wx, wy, wxs, wys,
    buf_a, buf_b, pair, outbox, wide, far, own_c, pick, rows, rows_nb, gmat, y_out, y_first, y_ref, yd_ref,
    in_sem, halo_send, halo_recv, a_send, a_recv, b_send, b_recv, set_send, set_recv,
    w_send, w_recv, g_send, g_recv, y_send, y_recv, pair_send, pair_recv, wide_send, wide_recv, far_send, far_recv,
):
    gx, gy, gz = lax.axis_index("gx"), lax.axis_index("gy"), lax.axis_index("gz")
    ngx, ngy = lax.axis_size("gx"), lax.axis_size("gy")
    me = gy * 2 + gz
    loads = [
        pltpu.make_async_copy(src, dst, in_sem.at[index])
        for index, (src, dst) in enumerate(
            [
                (own_in, own_ref), (perm_in, perm_ref), (b_in, r_ref), (w_in, w_ref),
                (cinv_in, cinv_ref), (sto_in, sto_ref), (mar_in, mar_ref),
            ]
        )
    ]
    for load in loads:
        load.start()

    def brick_peer(step):
        other = lax.rem(me + step, GROUP)
        return {"gy": other // 2, "gz": lax.rem(other, 2)}

    def line_peer(step):
        return {"gx": lax.rem(gx + step, GROUP)}

    barrier = pltpu.get_barrier_semaphore()
    for step in range(1, GROUP):
        pl.semaphore_signal(barrier, inc=1, device_id=brick_peer(step), device_id_type=MESH)
        pl.semaphore_signal(barrier, inc=1, device_id=line_peer(step), device_id_type=MESH)

    lane = lax.broadcasted_iota(jnp.int32, (8, 128), 1)
    row = lax.broadcasted_iota(jnp.int32, (8, 128), 0)
    lane_p = lax.broadcasted_iota(jnp.int32, (CX, CY), 1)
    row_p = lax.broadcasted_iota(jnp.int32, (CX, CY), 0)
    zero8 = jnp.zeros((8, 128), F32)
    zero_p = jnp.zeros((CX, CY), F32)
    partner = {"gz": 1 - gz}
    left, right = {"gx": lax.rem(gx + ngx - 1, ngx)}, {"gx": lax.rem(gx + 1, ngx)}
    down, up = {"gy": lax.rem(gy + ngy - 1, ngy)}, {"gy": lax.rem(gy + 1, ngy)}

    def remote(src, dst, send, recv, device):
        return pltpu.make_async_remote_copy(
            src_ref=src, dst_ref=dst, send_sem=send, recv_sem=recv, device_id=device, device_id_type=MESH
        )

    def halo_copies(e):
        return [
            remote(sz.at[e], hz.at[e], halo_send.at[e, 0], halo_recv.at[e, 0], partner),
            remote(sx.at[e, 0], hx.at[e, 1], halo_send.at[e, 1], halo_recv.at[e, 1], left),
            remote(sx.at[e, 1], hx.at[e, 0], halo_send.at[e, 2], halo_recv.at[e, 2], right),
            remote(sy.at[e, 0], hy.at[e, 1], halo_send.at[e, 3], halo_recv.at[e, 3], down),
            remote(sy.at[e, 1], hy.at[e, 0], halo_send.at[e, 4], halo_recv.at[e, 4], up),
        ]

    def start_all(copies):
        for copy in copies:
            copy.start()

    def recv_all(copies):
        for copy in copies:
            copy.wait_recv()

    def send_all(copies):
        for copy in copies:
            copy.wait_send()

    def columns(i, plane, low, high):
        for part in range(CX // 8):
            place = 8 * i + part
            piece = plane[8 * part : 8 * part + 8, :]
            low = jnp.where(lane == place, pltpu.roll(piece, place, 1) if place else piece, low)
            high = jnp.where(lane == place, pltpu.roll(piece, place + 1, 1), high)
        return low, high

    def pack(e, i, plane, low, high):
        if i == 0:
            sz[e] = plane
        if i == CZ - 1:
            sz[e] = jnp.where(gz == 0, plane, sz[e])
        sx[e, 0, i : i + 1, :] = plane[0:1, :]
        sx[e, 1, i : i + 1, :] = plane[CX - 1 : CX, :]
        low, high = columns(i, plane, low, high)
        if i == CZ - 1:
            sy[e, 0] = low
            sy[e, 1] = high
        return low, high

    def shifted(i, plane, xlow, xhigh, ylow, yhigh):
        parts_low, parts_high = [], []
        for part in range(CX // 8):
            place = 8 * i + part
            parts_low.append(pltpu.roll(ylow, (128 - place) % 128, 1) if place else ylow)
            parts_high.append(pltpu.roll(yhigh, 127 - place, 1))
        x_minus = jnp.where(row_p == 0, xlow[i : i + 1, :], pltpu.roll(plane, 1, 0))
        x_plus = jnp.where(row_p == CX - 1, xhigh[i : i + 1, :], pltpu.roll(plane, CX - 1, 0))
        y_minus = jnp.where(lane_p == 0, jnp.concatenate(parts_low, 0), pltpu.roll(plane, 1, 1))
        y_plus = jnp.where(lane_p == CY - 1, jnp.concatenate(parts_high, 0), pltpu.roll(plane, CY - 1, 1))
        return x_minus, x_plus, y_minus, y_plus

    def neighbours(i, padded, xlow, xhigh, ylow, yhigh):
        x_minus, x_plus, y_minus, y_plus = shifted(i, padded[i + 1], xlow, xhigh, ylow, yhigh)
        total = tz[i] * padded[i] + tz[i + 1] * padded[i + 2]
        total = total + txl[i] * x_minus + txh[i] * x_plus
        return total + tyl[i] * y_minus + tyh[i] * y_plus

    def a_copies():
        return [remote(buf_a.at[me], buf_a.at[me], a_send, a_recv, brick_peer(step)) for step in range(1, GROUP)]

    def b_copies():
        return [remote(buf_b.at[gx], buf_b.at[gx], b_send, b_recv, line_peer(step)) for step in range(1, GROUP)]

    a_part, b_part = buf_a.at[pl.ds(0, GROUP - 1)], buf_b.at[pl.ds(0, GROUP - 1)]
    a_all = remote(a_part, a_part, a_send, a_recv, brick_peer(1))
    b_all = remote(b_part, b_part, b_send, b_recv, line_peer(1))

    chip = gy * GROUP + gx
    cx, cy = lax.rem(gx, 4), gx // 4

    def chip_at(dz, dy, dx):
        return {"gx": lax.rem(cy + dy, 4) * 4 + lax.rem(cx + dx, 4), "gy": lax.rem(gy + dz, ngy)}

    def pair_copy(k):
        return remote(pair.at[k, gz], pair.at[k, gz], pair_send.at[k], pair_recv.at[k], partner)

    def far_start(k):
        source, target = outbox.at[k, pl.ds(0, 1), :], far.at[k, gz, pl.ds(chip, 1), :]
        for dz, dy, dx in FAR:
            for core in (gz, 1 - gz):
                device = dict(chip_at(dz, dy, dx), gz=core)
                remote(source, target, far_send.at[k], far_recv.at[k], device).start()

    def wide_start(k):
        line = wide.at[k, pl.ds(chip, 1), :]

        def send(dz, dy, dx):
            remote(line, line, wide_send.at[k], wide_recv.at[k], chip_at(dz, dy, dx)).start()

        for dy, dx in LAYER[5:]:
            send(4, dy, dx)

        def layers(skip):
            def layer(j, carry):
                off = (j + 1) // 2
                dz = jnp.where(lax.rem(j, 2) == 1, 4 - off, 4 + off)
                for dy, dx in LAYER[skip:]:
                    send(dz, dy, dx)
                return carry

            return layer

        lax.fori_loop(1, 3, layers(1), 0)
        lax.fori_loop(3, 7, layers(0), 0)
        for dy, dx in LAYER[:-1]:
            send(0, dy, dx)

    def wide_all(k):
        part = wide.at[k, pl.ds(0, CHIPS - 1 - len(FAR)), :]
        return remote(part, part, wide_send.at[k], wide_recv.at[k], right)

    def far_all(k):
        part = far.at[k, 0, pl.ds(0, 2 * len(FAR)), :]
        return remote(part, part, far_send.at[k], far_recv.at[k], right)

    def lane_sums(parts):
        stacked = zero8
        for index, part in enumerate(parts):
            stacked = jnp.where(row == index, jnp.sum(part, 0, keepdims=True), stacked)
        return jnp.sum(stacked, 1, keepdims=True)

    def coefficient_row(parts):
        return jnp.sum(jnp.where(lane == 8 * me + row, lane_sums(parts), 0.0), 0, keepdims=True)

    def scalar_row(parts):
        place = GROUP * lax.rem(gy + 1, ngy)
        return jnp.sum(jnp.where(lane == place + row, lane_sums(parts), 0.0), 0, keepdims=True)

    def exchange(k, message, middle):
        pair[k, gz] = message
        pair_copy(k).start()
        outbox[k, 0:1, :] = message
        far_start(k)
        middle()
        pair_copy(k).wait_recv()
        wide[k, pl.ds(chip, 1), :] = pair[k, 0] + pair[k, 1]
        wide_start(k)

    def exchanged(k):
        wide_all(k).wait_recv()
        far_all(k).wait_recv()
        block = lax.broadcasted_iota(jnp.int32, (GROUP, 128), 1) // GROUP
        coefficients, scalars = jnp.zeros((GROUP, 128), F32), jnp.zeros((GROUP, 128), F32)
        for index in range(CHIPS // GROUP):
            span = slice(GROUP * index, GROUP * index + GROUP)
            part = wide[k, span, :] + (far[k, 0, span, :] + far[k, 1, span, :])
            coefficients = jnp.where(block == index, part, coefficients)
            scalars = jnp.where(block == (index + 1) % (CHIPS // GROUP), part, scalars)
        line = jnp.sum(scalars, 0, keepdims=True)
        spot = lax.rem(lane[0:1, :], GROUP)
        sums = [jnp.sum(jnp.where(spot == index, line, 0.0), 1, keepdims=True) for index in range(3)]
        return coefficients, sums

    loads[0].wait()
    own_line = jnp.concatenate([own_ref[0, 0], jnp.zeros((1, 120), jnp.int32)], 1)
    own_rows = jnp.sum(jnp.where(lane == row, own_line, 0).astype(F32), 1, keepdims=True)
    own_c[gx] = jnp.broadcast_to(own_rows, (8, 128))
    own_lane = jnp.sum(jnp.where(lane == 8 * me + row, own_rows, 0.0), 0, keepdims=True)

    loads[1].wait()
    low, high = zero8, zero8
    for i in range(CZ):
        low, high = pack(E_PERM, i, perm_ref[i], low, high)
    for k in range(ITERS):
        wide[k] = jnp.zeros((CHIPS, 128), F32)
        for core in range(2):
            far[k, core] = jnp.zeros((CHIPS, 128), F32)
    loads[2].wait()
    loads[3].wait()
    parts = [zero8] * NV
    for i in range(CZ):
        source = r_ref[i]
        for index in range(NV):
            parts[index] = parts[index] + fold(w_ref[index, i] * source)
    buf_a[me] = jnp.concatenate([coefficient_row(parts), own_lane], 0)
    pl.semaphore_wait(barrier, 2 * (GROUP - 1))

    for step in range(1, GROUP):
        remote(own_c.at[gx], own_c.at[gx], set_send.at[0], set_recv.at[0], line_peer(step)).start()
    start_all(a_copies())
    start_all(halo_copies(E_PERM))

    for index in range(NV):
        low, high = zero8, zero8
        for i in range(CZ):
            plane = w_ref[index, i]
            wxs[0, index, i : i + 1, :] = plane[0:1, :]
            wxs[1, index, i : i + 1, :] = plane[CX - 1 : CX, :]
            low, high = columns(i, plane, low, high)
        wys[0, index] = low
        wys[1, index] = high
    w_copies = [
        remote(w_ref.at[:, (CZ - 1) * (1 - gz)], wz, w_send.at[0], w_recv.at[0], partner),
        remote(wxs.at[0], wx.at[1], w_send.at[1], w_recv.at[1], left),
        remote(wxs.at[1], wx.at[0], w_send.at[2], w_recv.at[2], right),
        remote(wys.at[0], wy.at[1], w_send.at[3], w_recv.at[3], down),
        remote(wys.at[1], wy.at[0], w_send.at[4], w_recv.at[4], up),
    ]
    start_all(w_copies)

    loads[5].wait()
    loads[6].wait()
    recv_all(halo_copies(E_PERM))
    in_left = jnp.where(gx > 0, 1.0, 0.0)
    in_right = jnp.where(gx < ngx - 1, 1.0, 0.0)
    in_down = jnp.where(gy > 0, 1.0, 0.0)
    in_up = jnp.where(gy < ngy - 1, 1.0, 0.0)
    in_low = jnp.where(gz > 0, 1.0, 0.0)
    p_xl, p_xh = hx[E_PERM, 0] * in_left, hx[E_PERM, 1] * in_right
    p_yl, p_yh = hy[E_PERM, 0] * in_down, hy[E_PERM, 1] * in_up
    tz[0] = conduct(perm_ref[0], hz[E_PERM] * in_low)
    tz[CZ] = conduct(perm_ref[CZ - 1], hz[E_PERM] * (1.0 - in_low))
    for i in range(1, CZ):
        tz[i] = conduct(perm_ref[i - 1], perm_ref[i])
    for plane in (0, CZ + 1):
        qpad[plane] = zero_p
        zpad[plane] = zero_p
    low, high = zero8, zero8
    for i in range(CZ):
        center = perm_ref[i]
        x_minus, x_plus, y_minus, y_plus = shifted(i, center, p_xl, p_xh, p_yl, p_yh)
        t_xl, t_xh = conduct(center, x_minus), conduct(center, x_plus)
        t_yl, t_yh = conduct(center, y_minus), conduct(center, y_plus)
        txl[i], txh[i], tyl[i], tyh[i] = t_xl, t_xh, t_yl, t_yh
        diagonal = sto_ref[i] + tz[i] + tz[i + 1] + t_xl + t_xh + t_yl + t_yh
        d_ref[i] = diagonal
        relax = RELAX / diagonal
        s_ref[i] = relax
        v = relax * r_ref[i]
        qpad[i + 1] = v
        low, high = pack(E_V, i, v, low, high)
    start_all(halo_copies(E_V))

    a_all.wait_recv()
    total = buf_a[0]
    for slot in range(1, GROUP):
        total = total + buf_a[slot]
    buf_b[gx] = total
    start_all(b_copies())

    loads[4].wait()
    owned = own_c.at[pl.ds(0, GROUP - 1)]
    own_all = remote(owned, owned, set_send.at[0], set_recv.at[0], right)
    own_all.wait_recv()
    wanted = own_c[...].reshape(GROUP * NV, 128).astype(jnp.int32)
    lane_w = lax.broadcasted_iota(jnp.int32, (GROUP * NV, 128), 1)
    one_hot = jnp.concatenate(
        [jnp.where(wanted == lane_w + 128 * part, 1.0, 0.0).astype(F32) for part in range(GROUP)], 1
    )
    picked = lax.dot_general(
        one_hot, cinv_ref[...], (((1,), (1,)), ((), ())),
        precision=lax.Precision.HIGHEST, preferred_element_type=F32,
    )
    pick[...] = picked.reshape(GROUP, NV, 128)
    for step in range(1, GROUP):
        other = lax.rem(gx + step, GROUP)
        remote(pick.at[other], rows.at[gx], set_send.at[1], set_recv.at[1], {"gx": other}).start()
    rows[gx] = pick[gx]

    keep = [mar_ref[0, 0, 0:1, side : side + 1].astype(F32) for side in range(6)]
    keep_z = jnp.where(gz > 0, keep[0], keep[1])
    halo_plane = (CZ + 1) * (1 - gz)

    def local_pass(e, out, e_out):
        recv_all(halo_copies(e))
        qpad[halo_plane] = hz[e] * keep_z
        q_xl, q_xh = hx[e, 0] * keep[2], hx[e, 1] * keep[3]
        q_yl, q_yh = hy[e, 0] * keep[4], hy[e, 1] * keep[5]
        low, high = zero8, zero8
        for i in range(CZ):
            value = 1.3 * qpad[i + 1] + s_ref[i] * neighbours(i, qpad, q_xl, q_xh, q_yl, q_yh)
            out[i] = value
            low, high = pack(e_out, i, value, low, high)
        start_all(halo_copies(e_out))

    local_pass(E_V, lv, E_LV)

    for i in range(CZ):
        x_ref[i] = zero_p
        p_ref[i] = zero_p
        ap_ref[i] = zero_p
        lqp[i] = zero_p
    lqpz[...] = zero_p
    for side in range(2):
        lqpx[side], lqpy[side] = zero8, zero8
    for place in range(6):
        yd_ref[place] = zero8

    got = rows.at[pl.ds(0, GROUP - 1)]
    rows_all = remote(got, got, set_send.at[1], set_recv.at[1], right)
    rows_all.wait_recv()
    g_copies = [
        remote(rows, rows_nb.at[place], g_send.at[place], g_recv.at[place], device)
        for place, device in ((0, partner), (2, left), (1, right), (4, down), (3, up))
    ]
    y_copies = [
        remote(y_out, y_first.at[place], y_send.at[place], y_recv.at[place], device)
        for place, device in ((0, partner), (2, left), (1, right), (4, down), (3, up))
    ]
    b_all.wait_recv()

    def in_order(source, target):
        order = buf_b[:, 1, :].astype(jnp.int32)
        for part in range(GROUP):
            index = jnp.broadcast_to(order[part : part + 1, :], (8, 128))
            inside, block = index & 127, index >> 7
            chosen = zero8
            for source_part in range(GROUP):
                moved = jnp.take_along_axis(source[source_part], inside, axis=1)
                chosen = jnp.where(block == source_part, moved, chosen)
            target[part] = chosen

    def coarse_solution(matrix, vector):
        total = zero8
        for part in range(GROUP):
            total = total + matrix[part] * vector[part : part + 1, :]
        return jnp.broadcast_to(jnp.sum(total, 1, keepdims=True), (8, 128))

    def z_faces():
        z, solved = lvz[...], y_ref[1]
        for index in range(NV):
            z = z + wz[index] * solved[index : index + 1, :]
        zpad[halo_plane] = z
        for base, vectors, target, first_place in ((lvx, wx, zx, 2), (lvy, wy, zy, 4)):
            for side in range(2):
                z, solved = base[side], y_ref[first_place + side]
                for index in range(NV):
                    z = z + vectors[side, index] * solved[index : index + 1, :]
                target[side] = z

    in_order(rows, gmat.at[0])
    y_own = coarse_solution(gmat.at[0], buf_b[:, 0, :])
    y_out[...] = y_own
    start_all(y_copies)
    start_all(g_copies)
    y_ref[0] = y_own
    rz_first = zero8
    for i in range(CZ):
        z = lv[i]
        for index in range(NV):
            z = z + w_ref[index, i] * y_own[index : index + 1, :]
        zpad[i + 1] = z
        rz_first = rz_first + fold(r_ref[i] * z)
    recv_all(halo_copies(E_LV))
    lvz[...] = hz[E_LV]
    for side in range(2):
        lvx[side], lvy[side] = hx[E_LV, side], hy[E_LV, side]
    recv_all(w_copies)
    recv_all(y_copies)
    for place in range(5):
        y_ref[place + 1] = y_first[place]
    z_faces()

    def image_pass(last):
        xl, xh, yl, yh = zx[0], zx[1], zy[0], zy[1]
        zaz, zap = zero8, zero8
        parts = [zero8] * NV
        for i in range(CZ):
            z = zpad[i + 1]
            az = d_ref[i] * z - neighbours(i, zpad, xl, xh, yl, yh)
            az_ref[i] = az
            zaz = zaz + fold(z * az)
            zap = zap + fold(z * ap_ref[i])
            if not last:
                for index in range(NV):
                    parts[index] = parts[index] + fold(w_ref[index, i] * az)
        return zaz, zap, parts

    def steps(rz, zaz, zap, rz_old, pap_old, first):
        beta = jnp.where(first, 0.0, rz / rz_old)
        pap = zaz + beta * (2.0 * zap + beta * pap_old)
        return beta, pap, rz / pap

    def iteration(k, carry):
        rz_part, rz_old, pap_old = carry
        e_q, e_l = E_LOOP + 2 * k, E_LOOP + 1 + 2 * k
        zaz, zap, parts = image_pass(False)
        message = coefficient_row(parts) + scalar_row([rz_part, zaz, zap])

        def send_q():
            low, high = zero8, zero8
            for i in range(CZ):
                q = s_ref[i] * az_ref[i]
                qpad[i + 1] = q
                low, high = pack(e_q, i, q, low, high)
            start_all(halo_copies(e_q))

        exchange(k, message, send_q)
        local_pass(e_q, lq, e_l)

        @pl.when(k == 0)
        def _():
            recv_all(g_copies)
            for place in range(5):
                in_order(rows_nb.at[place], gmat.at[place + 1])

        recv_all(halo_copies(e_l))
        fresh_c, sums = exchanged(k)
        rz, zaz, zap = sums
        beta, pap, alpha = steps(rz, zaz, zap, rz_old, pap_old, k == 0)
        for place in range(6):
            yd = coarse_solution(gmat.at[place], fresh_c) + beta * yd_ref[place]
            yd_ref[place] = yd
            y_ref[place] = y_ref[place] - alpha * yd
        y_own = y_ref[0]
        rz_part = zero8
        for i in range(CZ):
            p = zpad[i + 1] + beta * p_ref[i]
            ap = az_ref[i] + beta * ap_ref[i]
            p_ref[i], ap_ref[i] = p, ap
            x_ref[i] = x_ref[i] + alpha * p
            r = r_ref[i] - alpha * ap
            r_ref[i] = r
            lqd = lq[i] + beta * lqp[i]
            lqp[i] = lqd
            z = lv[i] - alpha * lqd
            lv[i] = z
            for index in range(NV):
                z = z + w_ref[index, i] * y_own[index : index + 1, :]
            zpad[i + 1] = z
            rz_part = rz_part + fold(r * z)
        for halo, old, base in ((hx, lqpx, lvx), (hy, lqpy, lvy)):
            for side in range(2):
                lqd = halo[e_l, side] + beta * old[side]
                old[side] = lqd
                base[side] = base[side] - alpha * lqd
        lqd = hz[e_l] + beta * lqpz[...]
        lqpz[...] = lqd
        lvz[...] = lvz[...] - alpha * lqd
        z_faces()
        return rz_part, rz, pap

    one = jnp.ones((1, 1), F32)
    rz_part, rz_old, pap_old = lax.fori_loop(0, ITERS - 1, iteration, (rz_first, one, one))
    zaz, zap, _ = image_pass(True)
    exchange(ITERS - 1, scalar_row([rz_part, zaz, zap]), lambda: None)
    _, sums = exchanged(ITERS - 1)
    beta, pap, alpha = steps(*sums, rz_old, pap_old, False)
    for i in range(CZ):
        x_ref[i] = x_ref[i] + alpha * (zpad[i + 1] + beta * p_ref[i])
        r_ref[i] = r_ref[i] - alpha * (az_ref[i] + beta * ap_ref[i])

    for e in range(HALOS):
        send_all(halo_copies(e))
    for k in range(ITERS):
        pair_copy(k).wait_send()
        wide_all(k).wait_send()
        far_all(k).wait_send()
    send_all([a_all, b_all, own_all, rows_all] + w_copies + g_copies + y_copies)


def local(right_side, permeability, storage, deflation, coarse_inverse, owners, margin):
    hbm = pl.BlockSpec(memory_space=pltpu.HBM)
    vmem = pl.BlockSpec(memory_space=pltpu.VMEM)
    shape = jax.ShapeDtypeStruct((CZ, CX, CY), F32)
    dma = pltpu.SemaphoreType.DMA

    def ram(*dims, dtype=F32):
        return pltpu.VMEM(dims, dtype)

    field, padded = ram(CZ, CX, CY), ram(CZ + 2, CX, CY)
    plane, ends = ram(CX, CY), ram(2, 8, 128)
    return pl.pallas_call(
        kernel,
        out_shape=(shape, shape),
        in_specs=[hbm] * 7,
        out_specs=(vmem, vmem),
        scratch_shapes=[
            field, field, ram(NV, CZ, CX, CY), ram(*coarse_inverse.shape),
            ram(*owners.shape, dtype=jnp.int32), ram(*margin.shape, dtype=jnp.int32),
            padded, padded, field, field, field, field, field, ram(CZ + 1, CX, CY),
            field, field, field, field, field, field, field,
            ram(HALOS, CX, CY), ram(HALOS, 2, 8, 128), ram(HALOS, 2, 8, 128),
            ram(HALOS, CX, CY), ram(HALOS, 2, 8, 128), ram(HALOS, 2, 8, 128),
            ends, ends, ends, ends, plane, ends, ends, plane, ends, ends,
            ram(NV, CX, CY), ram(2, NV, 8, 128), ram(2, NV, 8, 128), ram(2, NV, 8, 128), ram(2, NV, 8, 128),
            ram(GROUP, 2, 128), ram(GROUP, 2, 128), ram(ITERS, 2, 1, 128), ram(ITERS, 8, 128),
            ram(ITERS, CHIPS, 128), ram(ITERS, 2, CHIPS, 128),
            ram(GROUP, 8, 128), ram(GROUP, 8, 128), ram(GROUP, 8, 128), ram(5, GROUP, 8, 128),
            ram(6, GROUP, 8, 128), ram(8, 128), ram(5, 8, 128), ram(6, 8, 128), ram(6, 8, 128),
            dma((7,)), dma((HALOS, 5)), dma((HALOS, 5)), dma, dma, dma, dma, dma((2,)), dma((2,)),
            dma((5,)), dma((5,)), dma((5,)), dma((5,)), dma((5,)), dma((5,)),
            dma((ITERS,)), dma((ITERS,)), dma((ITERS,)), dma((ITERS,)), dma((ITERS,)), dma((ITERS,)),
        ],
        compiler_params=pltpu.CompilerParams(
            collective_id=0, has_side_effects=True, vmem_limit_bytes=62 * 1024 * 1024
        ),
    )(right_side, permeability, storage, deflation, coarse_inverse, owners, margin)


def solution(mesh):
    in_specs = (
        P("gz", "gx", "gy"),
        P("gz", "gx", "gy"),
        P("gz", "gx", "gy"),
        P(None, "gz", "gx", "gy"),
        P("gx", None),
        P("gz", "gx", "gy", None),
        P("gz", "gx", "gy", None),
    )
    out_specs = (P("gz", "gx", "gy"), P("gz", "gx", "gy"))
    return jax.shard_map(local, mesh=mesh, in_specs=in_specs, out_specs=out_specs, check_vma=False)
```

```python
import jax
import jax.numpy as jnp
from jax import lax
from jax.experimental import pallas as pl
from jax.experimental.pallas import tpu as pltpu
from jax.sharding import PartitionSpec as P

ITERS = 4
RELAX = 0.7
MESH = pl.DeviceIdType.MESH
F32 = jnp.float32
CZ, CX, CY, NV = 8, 64, 128, 8
GROUP = 16
CHIPS = 128
E_PERM, E_V, E_LV, E_LOOP = 0, 1, 2, 3
HALOS = E_LOOP + 2 * (ITERS - 1)
LAYER = sorted(
    [(a, b) for a in range(4) for b in range(4)], key=lambda t: -(min(t[0], 4 - t[0]) + min(t[1], 4 - t[1]))
)

FAR = [(4, dy, dx) for dy, dx in LAYER[:5]] + [(dz, 2, 2) for dz in (3, 5)]


def conduct(a, b):
    return 2.0 * a * b / jnp.maximum(a + b, 0.05)


def fold(plane):
    total = plane[0:8]
    for part in range(1, CX // 8):
        total = total + plane[8 * part : 8 * part + 8]
    return total


def kernel(
    b_in, perm_in, sto_in, w_in, cinv_in, own_in, mar_in,
    x_ref, r_ref, p_ref, ap_ref,
    perm_ref, sto_ref, w_ref, cinv_ref, own_ref, mar_ref,
    qpad, zpad, az_ref, d_ref, s_ref, tz, txl, txh, tyl, tyh, lv, lq, lqp,
    hz, hx, hy, sz, sx, sy, qx, qy, zx, zy, lvz, lvx, lvy, lqpz, lqpx, lqpy,
    wz, wx, wy, wxs, wys,
    buf_a, buf_b, pair, outbox, wide, far, own_c, pick, rows, rows_nb, gmat, split, y_out, y_first, y_ref, yd_ref,
    in_sem, halo_send, halo_recv, a_send, a_recv, b_send, b_recv, set_send, set_recv,
    w_send, w_recv, g_send, g_recv, y_send, y_recv, pair_send, pair_recv, wide_send, wide_recv, far_send, far_recv,
):
    gx, gy, gz = lax.axis_index("gx"), lax.axis_index("gy"), lax.axis_index("gz")
    ngx, ngy = lax.axis_size("gx"), lax.axis_size("gy")
    me = gy * 2 + gz
    loads = [
        pltpu.make_async_copy(src, dst, in_sem.at[index])
        for index, (src, dst) in enumerate(
            [
                (own_in, own_ref), (perm_in, perm_ref), (b_in, r_ref), (w_in, w_ref),
                (cinv_in, cinv_ref), (sto_in, sto_ref), (mar_in, mar_ref),
            ]
        )
    ]
    for load in loads:
        load.start()

    def brick_peer(step):
        other = lax.rem(me + step, GROUP)
        return {"gy": other // 2, "gz": lax.rem(other, 2)}

    def line_peer(step):
        return {"gx": lax.rem(gx + step, GROUP)}

    barrier = pltpu.get_barrier_semaphore()
    for step in range(1, GROUP):
        pl.semaphore_signal(barrier, inc=1, device_id=brick_peer(step), device_id_type=MESH)
        pl.semaphore_signal(barrier, inc=1, device_id=line_peer(step), device_id_type=MESH)

    lane = lax.broadcasted_iota(jnp.int32, (8, 128), 1)
    row = lax.broadcasted_iota(jnp.int32, (8, 128), 0)
    lane_p = lax.broadcasted_iota(jnp.int32, (CX, CY), 1)
    row_p = lax.broadcasted_iota(jnp.int32, (CX, CY), 0)
    zero8 = jnp.zeros((8, 128), F32)
    zero_p = jnp.zeros((CX, CY), F32)
    partner = {"gz": 1 - gz}
    left, right = {"gx": lax.rem(gx + ngx - 1, ngx)}, {"gx": lax.rem(gx + 1, ngx)}
    down, up = {"gy": lax.rem(gy + ngy - 1, ngy)}, {"gy": lax.rem(gy + 1, ngy)}

    def remote(src, dst, send, recv, device):
        return pltpu.make_async_remote_copy(
            src_ref=src, dst_ref=dst, send_sem=send, recv_sem=recv, device_id=device, device_id_type=MESH
        )

    def halo_copies(e):
        return [
            remote(sz.at[e], hz.at[e], halo_send.at[e, 0], halo_recv.at[e, 0], partner),
            remote(sx.at[e, 0], hx.at[e, 1], halo_send.at[e, 1], halo_recv.at[e, 1], left),
            remote(sx.at[e, 1], hx.at[e, 0], halo_send.at[e, 2], halo_recv.at[e, 2], right),
            remote(sy.at[e, 0], hy.at[e, 1], halo_send.at[e, 3], halo_recv.at[e, 3], down),
            remote(sy.at[e, 1], hy.at[e, 0], halo_send.at[e, 4], halo_recv.at[e, 4], up),
        ]

    def start_all(copies):
        for copy in copies:
            copy.start()

    def recv_all(copies):
        for copy in copies:
            copy.wait_recv()

    def send_all(copies):
        for copy in copies:
            copy.wait_send()

    def columns(i, plane, low, high):
        for part in range(CX // 8):
            place = 8 * i + part
            piece = plane[8 * part : 8 * part + 8, :]
            low = jnp.where(lane == place, pltpu.roll(piece, place, 1) if place else piece, low)
            high = jnp.where(lane == place, pltpu.roll(piece, place + 1, 1), high)
        return low, high

    def pack(e, i, plane, low, high):
        if i == 0:
            sz[e] = plane
        if i == CZ - 1:
            sz[e] = jnp.where(gz == 0, plane, sz[e])
        sx[e, 0, i : i + 1, :] = plane[0:1, :]
        sx[e, 1, i : i + 1, :] = plane[CX - 1 : CX, :]
        low, high = columns(i, plane, low, high)
        if i == CZ - 1:
            sy[e, 0] = low
            sy[e, 1] = high
        return low, high

    def shifted(i, plane, xlow, xhigh, ylow, yhigh):
        parts_low, parts_high = [], []
        for part in range(CX // 8):
            place = 8 * i + part
            parts_low.append(pltpu.roll(ylow, (128 - place) % 128, 1) if place else ylow)
            parts_high.append(pltpu.roll(yhigh, 127 - place, 1))
        x_minus = jnp.where(row_p == 0, xlow[i : i + 1, :], pltpu.roll(plane, 1, 0))
        x_plus = jnp.where(row_p == CX - 1, xhigh[i : i + 1, :], pltpu.roll(plane, CX - 1, 0))
        y_minus = jnp.where(lane_p == 0, jnp.concatenate(parts_low, 0), pltpu.roll(plane, 1, 1))
        y_plus = jnp.where(lane_p == CY - 1, jnp.concatenate(parts_high, 0), pltpu.roll(plane, CY - 1, 1))
        return x_minus, x_plus, y_minus, y_plus

    def neighbours(i, padded, xlow, xhigh, ylow, yhigh):
        x_minus, x_plus, y_minus, y_plus = shifted(i, padded[i + 1], xlow, xhigh, ylow, yhigh)
        total = tz[i] * padded[i] + tz[i + 1] * padded[i + 2]
        total = total + txl[i] * x_minus + txh[i] * x_plus
        return total + tyl[i] * y_minus + tyh[i] * y_plus

    def a_copies():
        return [remote(buf_a.at[me], buf_a.at[me], a_send, a_recv, brick_peer(step)) for step in range(1, GROUP)]

    def b_copies():
        return [remote(buf_b.at[gx], buf_b.at[gx], b_send, b_recv, line_peer(step)) for step in range(1, GROUP)]

    a_part, b_part = buf_a.at[pl.ds(0, GROUP - 1)], buf_b.at[pl.ds(0, GROUP - 1)]
    a_all = remote(a_part, a_part, a_send, a_recv, brick_peer(1))
    b_all = remote(b_part, b_part, b_send, b_recv, line_peer(1))

    chip = gy * GROUP + gx
    cx, cy = lax.rem(gx, 4), gx // 4

    def chip_at(dz, dy, dx):
        return {"gx": lax.rem(cy + dy, 4) * 4 + lax.rem(cx + dx, 4), "gy": lax.rem(gy + dz, ngy)}

    def pair_copy(k):
        return remote(pair.at[k, gz], pair.at[k, gz], pair_send.at[k], pair_recv.at[k], partner)

    def far_start(k):
        source, target = outbox.at[k, pl.ds(0, 1), :], far.at[k, gz, pl.ds(chip, 1), :]
        for dz, dy, dx in FAR:
            for core in (gz, 1 - gz):
                device = dict(chip_at(dz, dy, dx), gz=core)
                remote(source, target, far_send.at[k], far_recv.at[k], device).start()

    def wide_send_to(k, dz, offsets):
        line = wide.at[k, pl.ds(chip, 1), :]
        for dy, dx in offsets:
            remote(line, line, wide_send.at[k], wide_recv.at[k], chip_at(dz, dy, dx)).start()

    def wide_layers(k, first, last, offsets):
        def layer(j, carry):
            off = (j + 1) // 2
            wide_send_to(k, jnp.where(lax.rem(j, 2) == 1, 4 - off, 4 + off), offsets)
            return carry

        lax.fori_loop(first, last, layer, 0)

    def wide_start(k):
        wide_send_to(k, 4, LAYER[5:])
        wide_layers(k, 1, 3, LAYER[1:])
        wide_layers(k, 3, 7, LAYER)
        wide_send_to(k, 0, LAYER[:-1])

    def wide_all(k):
        part = wide.at[k, pl.ds(0, CHIPS - 1 - len(FAR)), :]
        return remote(part, part, wide_send.at[k], wide_recv.at[k], right)

    def far_all(k):
        part = far.at[k, 0, pl.ds(0, 2 * len(FAR)), :]
        return remote(part, part, far_send.at[k], far_recv.at[k], right)

    def lane_sums(parts):
        stacked = zero8
        for index, part in enumerate(parts):
            stacked = jnp.where(row == index, jnp.sum(part, 0, keepdims=True), stacked)
        return jnp.sum(stacked, 1, keepdims=True)

    def coefficient_row(parts):
        return jnp.sum(jnp.where(lane == 8 * me + row, lane_sums(parts), 0.0), 0, keepdims=True)

    def scalar_row(parts):
        place = GROUP * lax.rem(gy + 1, ngy)
        return jnp.sum(jnp.where(lane == place + row, lane_sums(parts), 0.0), 0, keepdims=True)

    def exchange(k, message):
        pair[k, gz] = message
        pair_copy(k).start()
        outbox[k, 0:1, :] = message
        far_start(k)
        pair_copy(k).wait_recv()
        wide[k, pl.ds(chip, 1), :] = pair[k, 0] + pair[k, 1]
        wide_start(k)

    def exchanged(k):
        wide_all(k).wait_recv()
        far_all(k).wait_recv()
        block = lax.broadcasted_iota(jnp.int32, (GROUP, 128), 1) // GROUP
        coefficients, scalars = jnp.zeros((GROUP, 128), F32), jnp.zeros((GROUP, 128), F32)
        for index in range(CHIPS // GROUP):
            span = slice(GROUP * index, GROUP * index + GROUP)
            part = wide[k, span, :] + (far[k, 0, span, :] + far[k, 1, span, :])
            coefficients = jnp.where(block == index, part, coefficients)
            scalars = jnp.where(block == (index + 1) % (CHIPS // GROUP), part, scalars)
        line = jnp.sum(scalars, 0, keepdims=True)
        spot = lax.rem(lane[0:1, :], GROUP)
        sums = [jnp.sum(jnp.where(spot == index, line, 0.0), 1, keepdims=True) for index in range(3)]
        return coefficients, sums

    loads[0].wait()
    own_line = jnp.concatenate([own_ref[0, 0], jnp.zeros((1, 120), jnp.int32)], 1)
    own_rows = jnp.sum(jnp.where(lane == row, own_line, 0).astype(F32), 1, keepdims=True)
    own_c[gx] = jnp.broadcast_to(own_rows, (8, 128))
    own_lane = jnp.sum(jnp.where(lane == 8 * me + row, own_rows, 0.0), 0, keepdims=True)

    loads[1].wait()
    low, high = zero8, zero8
    for i in range(CZ):
        low, high = pack(E_PERM, i, perm_ref[i], low, high)
    for k in range(ITERS):
        wide[k] = jnp.zeros((CHIPS, 128), F32)
        for core in range(2):
            far[k, core] = jnp.zeros((CHIPS, 128), F32)
    loads[2].wait()
    loads[3].wait()
    parts = [zero8] * NV
    for i in range(CZ):
        source = r_ref[i]
        for index in range(NV):
            parts[index] = parts[index] + fold(w_ref[index, i] * source)
    buf_a[me] = jnp.concatenate([coefficient_row(parts), own_lane], 0)
    loads[4].wait()
    for part in range(GROUP):
        span = slice(128 * part, 128 * part + 128)
        rest = cinv_ref[:, span]
        for level in range(3):
            piece = rest.astype(jnp.bfloat16)
            split[level, :, span] = piece
            rest = rest - piece.astype(F32)
    pl.semaphore_wait(barrier, 2 * (GROUP - 1))

    for step in range(1, GROUP):
        remote(own_c.at[gx], own_c.at[gx], set_send.at[0], set_recv.at[0], line_peer(step)).start()
    start_all(a_copies())
    start_all(halo_copies(E_PERM))

    for index in range(NV):
        low, high = zero8, zero8
        for i in range(CZ):
            plane = w_ref[index, i]
            wxs[0, index, i : i + 1, :] = plane[0:1, :]
            wxs[1, index, i : i + 1, :] = plane[CX - 1 : CX, :]
            low, high = columns(i, plane, low, high)
        wys[0, index] = low
        wys[1, index] = high
    w_copies = [
        remote(w_ref.at[:, (CZ - 1) * (1 - gz)], wz, w_send.at[0], w_recv.at[0], partner),
        remote(wxs.at[0], wx.at[1], w_send.at[1], w_recv.at[1], left),
        remote(wxs.at[1], wx.at[0], w_send.at[2], w_recv.at[2], right),
        remote(wys.at[0], wy.at[1], w_send.at[3], w_recv.at[3], down),
        remote(wys.at[1], wy.at[0], w_send.at[4], w_recv.at[4], up),
    ]
    start_all(w_copies)

    loads[5].wait()
    loads[6].wait()
    recv_all(halo_copies(E_PERM))
    in_left = jnp.where(gx > 0, 1.0, 0.0)
    in_right = jnp.where(gx < ngx - 1, 1.0, 0.0)
    in_down = jnp.where(gy > 0, 1.0, 0.0)
    in_up = jnp.where(gy < ngy - 1, 1.0, 0.0)
    in_low = jnp.where(gz > 0, 1.0, 0.0)
    p_xl, p_xh = hx[E_PERM, 0] * in_left, hx[E_PERM, 1] * in_right
    p_yl, p_yh = hy[E_PERM, 0] * in_down, hy[E_PERM, 1] * in_up
    tz[0] = conduct(perm_ref[0], hz[E_PERM] * in_low)
    tz[CZ] = conduct(perm_ref[CZ - 1], hz[E_PERM] * (1.0 - in_low))
    for i in range(1, CZ):
        tz[i] = conduct(perm_ref[i - 1], perm_ref[i])
    for plane in (0, CZ + 1):
        qpad[plane] = zero_p
        zpad[plane] = zero_p
    low, high = zero8, zero8
    for i in range(CZ):
        center = perm_ref[i]
        x_minus, x_plus, y_minus, y_plus = shifted(i, center, p_xl, p_xh, p_yl, p_yh)
        t_xl, t_xh = conduct(center, x_minus), conduct(center, x_plus)
        t_yl, t_yh = conduct(center, y_minus), conduct(center, y_plus)
        txl[i], txh[i], tyl[i], tyh[i] = t_xl, t_xh, t_yl, t_yh
        diagonal = sto_ref[i] + tz[i] + tz[i + 1] + t_xl + t_xh + t_yl + t_yh
        d_ref[i] = diagonal
        relax = RELAX / diagonal
        s_ref[i] = relax
        v = relax * r_ref[i]
        qpad[i + 1] = v
        low, high = pack(E_V, i, v, low, high)
    start_all(halo_copies(E_V))

    owned = own_c.at[pl.ds(0, GROUP - 1)]
    own_all = remote(owned, owned, set_send.at[0], set_recv.at[0], right)
    own_all.wait_recv()
    wanted = own_c[...].reshape(GROUP * NV, 128).astype(jnp.int32)
    lane_w = lax.broadcasted_iota(jnp.int32, (GROUP * NV, 128), 1)
    one_hot = jnp.concatenate(
        [jnp.where(wanted == lane_w + 128 * part, 1.0, 0.0).astype(jnp.bfloat16) for part in range(GROUP)], 1
    )
    picked = jnp.zeros((GROUP * NV, 128), F32)
    for level in (2, 1, 0):
        picked = picked + lax.dot_general(
            one_hot, split[level], (((1,), (1,)), ((), ())), preferred_element_type=F32
        )
    pick[...] = picked.reshape(GROUP, NV, 128)
    for step in range(1, GROUP):
        other = lax.rem(gx + step, GROUP)
        remote(pick.at[other], rows.at[gx], set_send.at[1], set_recv.at[1], {"gx": other}).start()
    rows[gx] = pick[gx]

    a_all.wait_recv()
    total = buf_a[0]
    for slot in range(1, GROUP):
        total = total + buf_a[slot]
    buf_b[gx] = total
    start_all(b_copies())

    keep = [mar_ref[0, 0, 0:1, side : side + 1].astype(F32) for side in range(6)]
    keep_z = jnp.where(gz > 0, keep[0], keep[1])
    halo_plane = (CZ + 1) * (1 - gz)

    def local_pass(e, out, e_out):
        recv_all(halo_copies(e))
        qpad[halo_plane] = hz[e] * keep_z
        q_xl, q_xh = hx[e, 0] * keep[2], hx[e, 1] * keep[3]
        q_yl, q_yh = hy[e, 0] * keep[4], hy[e, 1] * keep[5]
        low, high = zero8, zero8
        for i in range(CZ):
            value = 1.3 * qpad[i + 1] + s_ref[i] * neighbours(i, qpad, q_xl, q_xh, q_yl, q_yh)
            out[i] = value
            low, high = pack(e_out, i, value, low, high)
        start_all(halo_copies(e_out))

    local_pass(E_V, lv, E_LV)

    for i in range(CZ):
        x_ref[i] = zero_p
        p_ref[i] = zero_p
        ap_ref[i] = zero_p
        lqp[i] = zero_p
    lqpz[...] = zero_p
    for side in range(2):
        lqpx[side], lqpy[side] = zero8, zero8
    for place in range(6):
        yd_ref[place] = zero8

    got = rows.at[pl.ds(0, GROUP - 1)]
    rows_all = remote(got, got, set_send.at[1], set_recv.at[1], right)
    rows_all.wait_recv()
    g_copies = [
        remote(rows, rows_nb.at[place], g_send.at[place], g_recv.at[place], device)
        for place, device in ((0, partner), (2, left), (1, right), (4, down), (3, up))
    ]
    y_copies = [
        remote(y_out, y_first.at[place], y_send.at[place], y_recv.at[place], device)
        for place, device in ((0, partner), (2, left), (1, right), (4, down), (3, up))
    ]
    b_all.wait_recv()

    def in_order(source, target):
        order = buf_b[:, 1, :].astype(jnp.int32)
        for part in range(GROUP):
            index = jnp.broadcast_to(order[part : part + 1, :], (8, 128))
            inside, block = index & 127, index >> 7
            chosen = zero8
            for source_part in range(GROUP):
                moved = jnp.take_along_axis(source[source_part], inside, axis=1)
                chosen = jnp.where(block == source_part, moved, chosen)
            target[part] = chosen

    def coarse_solution(matrix, vector):
        total = zero8
        for part in range(GROUP):
            total = total + matrix[part] * vector[part : part + 1, :]
        return jnp.broadcast_to(jnp.sum(total, 1, keepdims=True), (8, 128))

    def z_faces():
        z, solved = lvz[...], y_ref[1]
        for index in range(NV):
            z = z + wz[index] * solved[index : index + 1, :]
        zpad[halo_plane] = z
        for base, vectors, target, first_place in ((lvx, wx, zx, 2), (lvy, wy, zy, 4)):
            for side in range(2):
                z, solved = base[side], y_ref[first_place + side]
                for index in range(NV):
                    z = z + vectors[side, index] * solved[index : index + 1, :]
                target[side] = z

    in_order(rows, gmat.at[0])
    y_own = coarse_solution(gmat.at[0], buf_b[:, 0, :])
    y_out[...] = y_own
    start_all(y_copies)
    start_all(g_copies)
    y_ref[0] = y_own
    rz_first = zero8
    for i in range(CZ):
        z = lv[i]
        for index in range(NV):
            z = z + w_ref[index, i] * y_own[index : index + 1, :]
        zpad[i + 1] = z
        rz_first = rz_first + fold(r_ref[i] * z)
    recv_all(halo_copies(E_LV))
    lvz[...] = hz[E_LV]
    for side in range(2):
        lvx[side], lvy[side] = hx[E_LV, side], hy[E_LV, side]
    recv_all(w_copies)
    recv_all(y_copies)
    for place in range(5):
        y_ref[place + 1] = y_first[place]
    z_faces()

    def image_pass(e_q):
        xl, xh, yl, yh = zx[0], zx[1], zy[0], zy[1]
        zaz, zap = zero8, zero8
        low, high = zero8, zero8
        parts = [zero8] * NV
        for i in range(CZ):
            z = zpad[i + 1]
            az = d_ref[i] * z - neighbours(i, zpad, xl, xh, yl, yh)
            az_ref[i] = az
            zaz = zaz + fold(z * az)
            zap = zap + fold(z * ap_ref[i])
            if e_q is not None:
                q = s_ref[i] * az
                qpad[i + 1] = q
                low, high = pack(e_q, i, q, low, high)
                for index in range(NV):
                    parts[index] = parts[index] + fold(w_ref[index, i] * az)
        if e_q is not None:
            start_all(halo_copies(e_q))
        return zaz, zap, parts

    def steps(rz, zaz, zap, rz_old, pap_old, first):
        beta = jnp.where(first, 0.0, rz / rz_old)
        pap = zaz + beta * (2.0 * zap + beta * pap_old)
        return beta, pap, rz / pap

    def iteration(k, carry):
        rz_part, rz_old, pap_old = carry
        e_q, e_l = E_LOOP + 2 * k, E_LOOP + 1 + 2 * k
        zaz, zap, parts = image_pass(e_q)
        exchange(k, coefficient_row(parts) + scalar_row([rz_part, zaz, zap]))
        local_pass(e_q, lq, e_l)

        @pl.when(k == 0)
        def _():
            recv_all(g_copies)
            for place in range(5):
                in_order(rows_nb.at[place], gmat.at[place + 1])

        fresh_c, sums = exchanged(k)
        rz, zaz, zap = sums
        beta, pap, alpha = steps(rz, zaz, zap, rz_old, pap_old, k == 0)
        for place in range(6):
            yd = coarse_solution(gmat.at[place], fresh_c) + beta * yd_ref[place]
            yd_ref[place] = yd
            y_ref[place] = y_ref[place] - alpha * yd
        y_own = y_ref[0]
        rz_part = zero8
        for i in range(CZ):
            p = zpad[i + 1] + beta * p_ref[i]
            ap = az_ref[i] + beta * ap_ref[i]
            p_ref[i], ap_ref[i] = p, ap
            x_ref[i] = x_ref[i] + alpha * p
            r = r_ref[i] - alpha * ap
            r_ref[i] = r
            lqd = lq[i] + beta * lqp[i]
            lqp[i] = lqd
            z = lv[i] - alpha * lqd
            lv[i] = z
            for index in range(NV):
                z = z + w_ref[index, i] * y_own[index : index + 1, :]
            zpad[i + 1] = z
            rz_part = rz_part + fold(r * z)
        recv_all(halo_copies(e_l))
        for halo, old, base in ((hx, lqpx, lvx), (hy, lqpy, lvy)):
            for side in range(2):
                lqd = halo[e_l, side] + beta * old[side]
                old[side] = lqd
                base[side] = base[side] - alpha * lqd
        lqd = hz[e_l] + beta * lqpz[...]
        lqpz[...] = lqd
        lvz[...] = lvz[...] - alpha * lqd
        z_faces()
        return rz_part, rz, pap

    one = jnp.ones((1, 1), F32)
    rz_part, rz_old, pap_old = lax.fori_loop(0, ITERS - 1, iteration, (rz_first, one, one))
    zaz, zap, _ = image_pass(None)
    exchange(ITERS - 1, scalar_row([rz_part, zaz, zap]))
    _, sums = exchanged(ITERS - 1)
    beta, pap, alpha = steps(*sums, rz_old, pap_old, False)
    for i in range(CZ):
        p_ref[i] = alpha * (zpad[i + 1] + beta * p_ref[i])
        ap_ref[i] = alpha * (az_ref[i] + beta * ap_ref[i])

    for e in range(HALOS):
        send_all(halo_copies(e))
    for k in range(ITERS):
        pair_copy(k).wait_send()
        wide_all(k).wait_send()
        far_all(k).wait_send()
    send_all([a_all, b_all, own_all, rows_all] + w_copies + g_copies + y_copies)


def local(right_side, permeability, storage, deflation, coarse_inverse, owners, margin):
    hbm = pl.BlockSpec(memory_space=pltpu.HBM)
    vmem = pl.BlockSpec(memory_space=pltpu.VMEM)
    shape = jax.ShapeDtypeStruct((CZ, CX, CY), F32)
    dma = pltpu.SemaphoreType.DMA

    def ram(*dims, dtype=F32):
        return pltpu.VMEM(dims, dtype)

    field, padded = ram(CZ, CX, CY), ram(CZ + 2, CX, CY)
    plane, ends = ram(CX, CY), ram(2, 8, 128)
    before, rest, last_step, last_image = pl.pallas_call(
        kernel,
        out_shape=(shape,) * 4,
        in_specs=[hbm] * 7,
        out_specs=(vmem,) * 4,
        scratch_shapes=[
            field, field, ram(NV, CZ, CX, CY), ram(*coarse_inverse.shape),
            ram(*owners.shape, dtype=jnp.int32), ram(*margin.shape, dtype=jnp.int32),
            padded, padded, field, field, field, ram(CZ + 1, CX, CY),
            field, field, field, field, field, field, field,
            ram(HALOS, CX, CY), ram(HALOS, 2, 8, 128), ram(HALOS, 2, 8, 128),
            ram(HALOS, CX, CY), ram(HALOS, 2, 8, 128), ram(HALOS, 2, 8, 128),
            ends, ends, ends, ends, plane, ends, ends, plane, ends, ends,
            ram(NV, CX, CY), ram(2, NV, 8, 128), ram(2, NV, 8, 128), ram(2, NV, 8, 128), ram(2, NV, 8, 128),
            ram(GROUP, 2, 128), ram(GROUP, 2, 128), ram(ITERS, 2, 1, 128), ram(ITERS, 8, 128),
            ram(ITERS, CHIPS, 128), ram(ITERS, 2, CHIPS, 128),
            ram(GROUP, 8, 128), ram(GROUP, 8, 128), ram(GROUP, 8, 128), ram(5, GROUP, 8, 128),
            ram(6, GROUP, 8, 128), ram(3, *coarse_inverse.shape, dtype=jnp.bfloat16), ram(8, 128), ram(5, 8, 128), ram(6, 8, 128), ram(6, 8, 128),
            dma((7,)), dma((HALOS, 5)), dma((HALOS, 5)), dma, dma, dma, dma, dma((2,)), dma((2,)),
            dma((5,)), dma((5,)), dma((5,)), dma((5,)), dma((5,)), dma((5,)),
            dma((ITERS,)), dma((ITERS,)), dma((ITERS,)), dma((ITERS,)), dma((ITERS,)), dma((ITERS,)),
        ],
        compiler_params=pltpu.CompilerParams(
            collective_id=0, has_side_effects=True, vmem_limit_bytes=62 * 1024 * 1024
        ),
    )(right_side, permeability, storage, deflation, coarse_inverse, owners, margin)
    return before + last_step, rest - last_image


def solution(mesh):
    in_specs = (
        P("gz", "gx", "gy"),
        P("gz", "gx", "gy"),
        P("gz", "gx", "gy"),
        P(None, "gz", "gx", "gy"),
        P("gx", None),
        P("gz", "gx", "gy", None),
        P("gz", "gx", "gy", None),
    )
    out_specs = (P("gz", "gx", "gy"), P("gz", "gx", "gy"))
    return jax.shard_map(local, mesh=mesh, in_specs=in_specs, out_specs=out_specs, check_vma=False)
```

```python
import jax
import jax.numpy as jnp
from jax import lax
from jax.experimental import pallas as pl
from jax.experimental.pallas import tpu as pltpu
from jax.sharding import PartitionSpec as P

ITERS = 4
RELAX = 0.7
MESH = pl.DeviceIdType.MESH
F32 = jnp.float32
CZ, CX, CY, NV = 8, 64, 128, 8
GROUP = 16
CHIPS = 128
E_PERM, E_V, E_LV, E_LOOP = 0, 1, 2, 3
HALOS = E_LOOP + 2 * (ITERS - 1)
LAYER = sorted(
    [(a, b) for a in range(4) for b in range(4)], key=lambda t: -(min(t[0], 4 - t[0]) + min(t[1], 4 - t[1]))
)

FAR = [(4, dy, dx) for dy, dx in LAYER[:5]] + [(dz, 2, 2) for dz in (3, 5)]


def conduct(a, b):
    return 2.0 * a * b / jnp.maximum(a + b, 0.05)


def fold(plane):
    total = plane[0:8]
    for part in range(1, CX // 8):
        total = total + plane[8 * part : 8 * part + 8]
    return total


def kernel(
    b_in, perm_in, sto_in, w_in, cinv_in, own_in, mar_in,
    x_ref, r_ref, p_ref, ap_ref,
    perm_ref, sto_ref, w_ref, cinv_ref, own_ref, mar_ref,
    qpad, zpad, az_ref, d_ref, s_ref, tz, txl, txh, tyl, tyh, lv, lq, lqp,
    hz, hx, hy, sz, sx, sy, qx, qy, zx, zy, lvz, lvx, lvy, lqpz, lqpx, lqpy,
    wz, wx, wy, wxs, wys,
    buf_a, buf_b, pair, outbox, wide, far, own_c, pick, rows, rows_nb, gmat, split, y_out, y_first, y_ref, yd_ref,
    in_sem, halo_send, halo_recv, a_send, a_recv, b_send, b_recv, set_send, set_recv,
    w_send, w_recv, g_send, g_recv, y_send, y_recv, pair_send, pair_recv, wide_send, wide_recv, far_send, far_recv,
):
    gx, gy, gz = lax.axis_index("gx"), lax.axis_index("gy"), lax.axis_index("gz")
    ngx, ngy = lax.axis_size("gx"), lax.axis_size("gy")
    me = gy * 2 + gz
    loads = [
        pltpu.make_async_copy(src, dst, in_sem.at[index])
        for index, (src, dst) in enumerate(
            [
                (own_in, own_ref), (perm_in, perm_ref), (b_in, r_ref), (w_in, w_ref),
                (cinv_in, cinv_ref), (sto_in, sto_ref), (mar_in, mar_ref),
            ]
        )
    ]
    for load in loads:
        load.start()

    def brick_peer(step):
        other = lax.rem(me + step, GROUP)
        return {"gy": other // 2, "gz": lax.rem(other, 2)}

    def line_peer(step):
        return {"gx": lax.rem(gx + step, GROUP)}

    barrier = pltpu.get_barrier_semaphore()
    for step in range(1, GROUP):
        pl.semaphore_signal(barrier, inc=1, device_id=brick_peer(step), device_id_type=MESH)
        pl.semaphore_signal(barrier, inc=1, device_id=line_peer(step), device_id_type=MESH)

    lane = lax.broadcasted_iota(jnp.int32, (8, 128), 1)
    row = lax.broadcasted_iota(jnp.int32, (8, 128), 0)
    lane_p = lax.broadcasted_iota(jnp.int32, (CX, CY), 1)
    row_p = lax.broadcasted_iota(jnp.int32, (CX, CY), 0)
    zero8 = jnp.zeros((8, 128), F32)
    zero_p = jnp.zeros((CX, CY), F32)
    partner = {"gz": 1 - gz}
    left, right = {"gx": lax.rem(gx + ngx - 1, ngx)}, {"gx": lax.rem(gx + 1, ngx)}
    down, up = {"gy": lax.rem(gy + ngy - 1, ngy)}, {"gy": lax.rem(gy + 1, ngy)}

    def remote(src, dst, send, recv, device):
        return pltpu.make_async_remote_copy(
            src_ref=src, dst_ref=dst, send_sem=send, recv_sem=recv, device_id=device, device_id_type=MESH
        )

    def halo_copies(e):
        return [
            remote(sz.at[e], hz.at[e], halo_send.at[e, 0], halo_recv.at[e, 0], partner),
            remote(sx.at[e, 0], hx.at[e, 1], halo_send.at[e, 1], halo_recv.at[e, 1], left),
            remote(sx.at[e, 1], hx.at[e, 0], halo_send.at[e, 2], halo_recv.at[e, 2], right),
            remote(sy.at[e, 0], hy.at[e, 1], halo_send.at[e, 3], halo_recv.at[e, 3], down),
            remote(sy.at[e, 1], hy.at[e, 0], halo_send.at[e, 4], halo_recv.at[e, 4], up),
        ]

    def start_all(copies):
        for copy in copies:
            copy.start()

    def recv_all(copies):
        for copy in copies:
            copy.wait_recv()

    def send_all(copies):
        for copy in copies:
            copy.wait_send()

    def columns(i, plane, low, high):
        for part in range(CX // 8):
            place = 8 * i + part
            piece = plane[8 * part : 8 * part + 8, :]
            low = jnp.where(lane == place, pltpu.roll(piece, place, 1) if place else piece, low)
            high = jnp.where(lane == place, pltpu.roll(piece, place + 1, 1), high)
        return low, high

    def pack(e, i, plane, low, high):
        if i == 0:
            sz[e] = plane
        if i == CZ - 1:
            sz[e] = jnp.where(gz == 0, plane, sz[e])
        sx[e, 0, i : i + 1, :] = plane[0:1, :]
        sx[e, 1, i : i + 1, :] = plane[CX - 1 : CX, :]
        low, high = columns(i, plane, low, high)
        if i == CZ - 1:
            sy[e, 0] = low
            sy[e, 1] = high
        return low, high

    def shifted(i, plane, xlow, xhigh, ylow, yhigh):
        parts_low, parts_high = [], []
        for part in range(CX // 8):
            place = 8 * i + part
            parts_low.append(pltpu.roll(ylow, (128 - place) % 128, 1) if place else ylow)
            parts_high.append(pltpu.roll(yhigh, 127 - place, 1))
        x_minus = jnp.where(row_p == 0, xlow[i : i + 1, :], pltpu.roll(plane, 1, 0))
        x_plus = jnp.where(row_p == CX - 1, xhigh[i : i + 1, :], pltpu.roll(plane, CX - 1, 0))
        y_minus = jnp.where(lane_p == 0, jnp.concatenate(parts_low, 0), pltpu.roll(plane, 1, 1))
        y_plus = jnp.where(lane_p == CY - 1, jnp.concatenate(parts_high, 0), pltpu.roll(plane, CY - 1, 1))
        return x_minus, x_plus, y_minus, y_plus

    def neighbours(i, padded, xlow, xhigh, ylow, yhigh):
        x_minus, x_plus, y_minus, y_plus = shifted(i, padded[i + 1], xlow, xhigh, ylow, yhigh)
        total = tz[i] * padded[i] + tz[i + 1] * padded[i + 2]
        total = total + txl[i] * x_minus + txh[i] * x_plus
        return total + tyl[i] * y_minus + tyh[i] * y_plus

    def a_copies():
        return [remote(buf_a.at[me], buf_a.at[me], a_send, a_recv, brick_peer(step)) for step in range(1, GROUP)]

    def b_copies():
        return [remote(buf_b.at[gx], buf_b.at[gx], b_send, b_recv, line_peer(step)) for step in range(1, GROUP)]

    a_part, b_part = buf_a.at[pl.ds(0, GROUP - 1)], buf_b.at[pl.ds(0, GROUP - 1)]
    a_all = remote(a_part, a_part, a_send, a_recv, brick_peer(1))
    b_all = remote(b_part, b_part, b_send, b_recv, line_peer(1))

    chip = gy * GROUP + gx
    cx, cy = lax.rem(gx, 4), gx // 4

    def chip_at(dz, dy, dx):
        return {"gx": lax.rem(cy + dy, 4) * 4 + lax.rem(cx + dx, 4), "gy": lax.rem(gy + dz, ngy)}

    def pair_copy(k):
        return remote(pair.at[k, gz], pair.at[k, gz], pair_send.at[k], pair_recv.at[k], partner)

    def far_start(k):
        source, target = outbox.at[k, pl.ds(0, 1), :], far.at[k, gz, pl.ds(chip, 1), :]
        for dz, dy, dx in FAR:
            for core in (gz, 1 - gz):
                device = dict(chip_at(dz, dy, dx), gz=core)
                remote(source, target, far_send.at[k], far_recv.at[k], device).start()

    def wide_send_to(k, dz, offsets):
        line = wide.at[k, pl.ds(chip, 1), :]
        for dy, dx in offsets:
            remote(line, line, wide_send.at[k], wide_recv.at[k], chip_at(dz, dy, dx)).start()

    def wide_layers(k, first, last, offsets):
        def layer(j, carry):
            off = (j + 1) // 2
            wide_send_to(k, jnp.where(lax.rem(j, 2) == 1, 4 - off, 4 + off), offsets)
            return carry

        lax.fori_loop(first, last, layer, 0)

    def wide_start(k):
        wide_send_to(k, 4, LAYER[5:])
        wide_layers(k, 1, 3, LAYER[1:])
        wide_layers(k, 3, 7, LAYER)
        wide_send_to(k, 0, LAYER[:-1])

    def wide_all(k):
        part = wide.at[k, pl.ds(0, CHIPS - 1 - len(FAR)), :]
        return remote(part, part, wide_send.at[k], wide_recv.at[k], right)

    def far_all(k):
        part = far.at[k, 0, pl.ds(0, 2 * len(FAR)), :]
        return remote(part, part, far_send.at[k], far_recv.at[k], right)

    def lane_sums(parts):
        stacked = zero8
        for index, part in enumerate(parts):
            stacked = jnp.where(row == index, jnp.sum(part, 0, keepdims=True), stacked)
        return jnp.sum(stacked, 1, keepdims=True)

    def coefficient_row(parts):
        return jnp.sum(jnp.where(lane == 8 * me + row, lane_sums(parts), 0.0), 0, keepdims=True)

    def scalar_row(parts):
        place = GROUP * lax.rem(gy + 1, ngy)
        return jnp.sum(jnp.where(lane == place + row, lane_sums(parts), 0.0), 0, keepdims=True)

    def exchange(k, message):
        pair[k, gz] = message
        pair_copy(k).start()
        outbox[k, 0:1, :] = message
        far_start(k)
        pair_copy(k).wait_recv()
        wide[k, pl.ds(chip, 1), :] = pair[k, 0] + pair[k, 1]
        wide_start(k)

    def exchanged(k):
        wide_all(k).wait_recv()
        far_all(k).wait_recv()
        block = lax.broadcasted_iota(jnp.int32, (GROUP, 128), 1) // GROUP
        coefficients, scalars = jnp.zeros((GROUP, 128), F32), jnp.zeros((GROUP, 128), F32)
        for index in range(CHIPS // GROUP):
            span = slice(GROUP * index, GROUP * index + GROUP)
            part = wide[k, span, :] + (far[k, 0, span, :] + far[k, 1, span, :])
            coefficients = jnp.where(block == index, part, coefficients)
            scalars = jnp.where(block == (index + 1) % (CHIPS // GROUP), part, scalars)
        line = jnp.sum(scalars, 0, keepdims=True)
        spot = lax.rem(lane[0:1, :], GROUP)
        sums = [jnp.sum(jnp.where(spot == index, line, 0.0), 1, keepdims=True) for index in range(3)]
        return coefficients, sums

    loads[0].wait()
    own_line = jnp.concatenate([own_ref[0, 0], jnp.zeros((1, 120), jnp.int32)], 1)
    own_rows = jnp.sum(jnp.where(lane == row, own_line, 0).astype(F32), 1, keepdims=True)
    own_c[gx] = jnp.broadcast_to(own_rows, (8, 128))
    own_lane = jnp.sum(jnp.where(lane == 8 * me + row, own_rows, 0.0), 0, keepdims=True)

    loads[1].wait()
    low, high = zero8, zero8
    for i in range(CZ):
        low, high = pack(E_PERM, i, perm_ref[i], low, high)
    for k in range(ITERS):
        wide[k] = jnp.zeros((CHIPS, 128), F32)
        for core in range(2):
            far[k, core] = jnp.zeros((CHIPS, 128), F32)
    loads[2].wait()
    loads[3].wait()
    parts = [zero8] * NV
    for i in range(CZ):
        source = r_ref[i]
        for index in range(NV):
            parts[index] = parts[index] + fold(w_ref[index, i] * source)
    buf_a[me] = jnp.concatenate([coefficient_row(parts), own_lane], 0)
    loads[4].wait()
    for part in range(GROUP):
        span = slice(128 * part, 128 * part + 128)
        rest = cinv_ref[:, span]
        for level in range(3):
            piece = rest.astype(jnp.bfloat16)
            split[level, :, span] = piece
            rest = rest - piece.astype(F32)
    pl.semaphore_wait(barrier, 2 * (GROUP - 1))

    for step in range(1, GROUP):
        remote(own_c.at[gx], own_c.at[gx], set_send.at[0], set_recv.at[0], line_peer(step)).start()
    start_all(a_copies())
    start_all(halo_copies(E_PERM))

    for index in range(NV):
        low, high = zero8, zero8
        for i in range(CZ):
            plane = w_ref[index, i]
            wxs[0, index, i : i + 1, :] = plane[0:1, :]
            wxs[1, index, i : i + 1, :] = plane[CX - 1 : CX, :]
            low, high = columns(i, plane, low, high)
        wys[0, index] = low
        wys[1, index] = high
    w_copies = [
        remote(w_ref.at[:, (CZ - 1) * (1 - gz)], wz, w_send.at[0], w_recv.at[0], partner),
        remote(wxs.at[0], wx.at[1], w_send.at[1], w_recv.at[1], left),
        remote(wxs.at[1], wx.at[0], w_send.at[2], w_recv.at[2], right),
        remote(wys.at[0], wy.at[1], w_send.at[3], w_recv.at[3], down),
        remote(wys.at[1], wy.at[0], w_send.at[4], w_recv.at[4], up),
    ]
    start_all(w_copies)

    loads[5].wait()
    loads[6].wait()
    recv_all(halo_copies(E_PERM))
    in_left = jnp.where(gx > 0, 1.0, 0.0)
    in_right = jnp.where(gx < ngx - 1, 1.0, 0.0)
    in_down = jnp.where(gy > 0, 1.0, 0.0)
    in_up = jnp.where(gy < ngy - 1, 1.0, 0.0)
    in_low = jnp.where(gz > 0, 1.0, 0.0)
    p_xl, p_xh = hx[E_PERM, 0] * in_left, hx[E_PERM, 1] * in_right
    p_yl, p_yh = hy[E_PERM, 0] * in_down, hy[E_PERM, 1] * in_up
    tz[0] = conduct(perm_ref[0], hz[E_PERM] * in_low)
    tz[CZ] = conduct(perm_ref[CZ - 1], hz[E_PERM] * (1.0 - in_low))
    for i in range(1, CZ):
        tz[i] = conduct(perm_ref[i - 1], perm_ref[i])
    for plane in (0, CZ + 1):
        qpad[plane] = zero_p
        zpad[plane] = zero_p
    low, high = zero8, zero8
    for i in range(CZ):
        center = perm_ref[i]
        x_minus, x_plus, y_minus, y_plus = shifted(i, center, p_xl, p_xh, p_yl, p_yh)
        t_xl, t_xh = conduct(center, x_minus), conduct(center, x_plus)
        t_yl, t_yh = conduct(center, y_minus), conduct(center, y_plus)
        txl[i], txh[i], tyl[i], tyh[i] = t_xl, t_xh, t_yl, t_yh
        diagonal = sto_ref[i] + tz[i] + tz[i + 1] + t_xl + t_xh + t_yl + t_yh
        d_ref[i] = diagonal
        relax = RELAX / diagonal
        s_ref[i] = relax
        v = relax * r_ref[i]
        qpad[i + 1] = v
        low, high = pack(E_V, i, v, low, high)
    start_all(halo_copies(E_V))

    owned = own_c.at[pl.ds(0, GROUP - 1)]
    own_all = remote(owned, owned, set_send.at[0], set_recv.at[0], right)
    own_all.wait_recv()
    wanted = own_c[...].reshape(GROUP * NV, 128).astype(jnp.int32)
    lane_w = lax.broadcasted_iota(jnp.int32, (GROUP * NV, 128), 1)
    one_hot = jnp.concatenate(
        [jnp.where(wanted == lane_w + 128 * part, 1.0, 0.0).astype(jnp.bfloat16) for part in range(GROUP)], 1
    )
    picked = jnp.zeros((GROUP * NV, 128), F32)
    for level in (2, 1, 0):
        picked = picked + lax.dot_general(
            one_hot, split[level], (((1,), (1,)), ((), ())), preferred_element_type=F32
        )
    pick[...] = picked.reshape(GROUP, NV, 128)
    for step in range(1, GROUP):
        other = lax.rem(gx + step, GROUP)
        remote(pick.at[other], rows.at[gx], set_send.at[1], set_recv.at[1], {"gx": other}).start()
    rows[gx] = pick[gx]

    a_all.wait_recv()
    total = buf_a[0]
    for slot in range(1, GROUP):
        total = total + buf_a[slot]
    buf_b[gx] = total
    start_all(b_copies())

    keep = [mar_ref[0, 0, 0:1, side : side + 1].astype(F32) for side in range(6)]
    keep_z = jnp.where(gz > 0, keep[0], keep[1])
    halo_plane = (CZ + 1) * (1 - gz)

    def local_pass(e, out, e_out):
        recv_all(halo_copies(e))
        qpad[halo_plane] = hz[e] * keep_z
        q_xl, q_xh = hx[e, 0] * keep[2], hx[e, 1] * keep[3]
        q_yl, q_yh = hy[e, 0] * keep[4], hy[e, 1] * keep[5]
        low, high = zero8, zero8
        for i in range(CZ):
            value = 1.3 * qpad[i + 1] + s_ref[i] * neighbours(i, qpad, q_xl, q_xh, q_yl, q_yh)
            out[i] = value
            low, high = pack(e_out, i, value, low, high)
        start_all(halo_copies(e_out))

    local_pass(E_V, lv, E_LV)

    for i in range(CZ):
        x_ref[i] = zero_p
        p_ref[i] = zero_p
        ap_ref[i] = zero_p
        lqp[i] = zero_p
    lqpz[...] = zero_p
    for side in range(2):
        lqpx[side], lqpy[side] = zero8, zero8
    for place in range(6):
        yd_ref[place] = zero8

    got = rows.at[pl.ds(0, GROUP - 1)]
    rows_all = remote(got, got, set_send.at[1], set_recv.at[1], right)
    rows_all.wait_recv()
    g_copies = [
        remote(rows, rows_nb.at[place], g_send.at[place], g_recv.at[place], device)
        for place, device in ((0, partner), (2, left), (1, right), (4, down), (3, up))
    ]
    y_copies = [
        remote(y_out, y_first.at[place], y_send.at[place], y_recv.at[place], device)
        for place, device in ((0, partner), (2, left), (1, right), (4, down), (3, up))
    ]
    b_all.wait_recv()

    def in_order(source, target):
        order = buf_b[:, 1, :].astype(jnp.int32)
        for part in range(GROUP):
            index = jnp.broadcast_to(order[part : part + 1, :], (8, 128))
            inside, block = index & 127, index >> 7
            chosen = zero8
            for source_part in range(GROUP):
                moved = jnp.take_along_axis(source[source_part], inside, axis=1)
                chosen = jnp.where(block == source_part, moved, chosen)
            target[part] = chosen

    def coarse_solution(matrix, vector):
        total = zero8
        for part in range(GROUP):
            total = total + matrix[part] * vector[part : part + 1, :]
        return jnp.broadcast_to(jnp.sum(total, 1, keepdims=True), (8, 128))

    def z_faces():
        z, solved = lvz[...], y_ref[1]
        for index in range(NV):
            z = z + wz[index] * solved[index : index + 1, :]
        zpad[halo_plane] = z
        for base, vectors, target, first_place in ((lvx, wx, zx, 2), (lvy, wy, zy, 4)):
            for side in range(2):
                z, solved = base[side], y_ref[first_place + side]
                for index in range(NV):
                    z = z + vectors[side, index] * solved[index : index + 1, :]
                target[side] = z

    in_order(rows, gmat.at[0])
    y_own = coarse_solution(gmat.at[0], buf_b[:, 0, :])
    y_out[...] = y_own
    start_all(y_copies)
    start_all(g_copies)
    y_ref[0] = y_own
    rz_first = zero8
    for i in range(CZ):
        z = lv[i]
        for index in range(NV):
            z = z + w_ref[index, i] * y_own[index : index + 1, :]
        zpad[i + 1] = z
        rz_first = rz_first + fold(r_ref[i] * z)
    recv_all(halo_copies(E_LV))
    lvz[...] = hz[E_LV]
    for side in range(2):
        lvx[side], lvy[side] = hx[E_LV, side], hy[E_LV, side]
    recv_all(w_copies)
    recv_all(y_copies)
    for place in range(5):
        y_ref[place + 1] = y_first[place]
    z_faces()

    def image_pass(e_q):
        xl, xh, yl, yh = zx[0], zx[1], zy[0], zy[1]
        zaz, zap = zero8, zero8
        low, high = zero8, zero8
        parts = [zero8] * NV
        for i in range(CZ):
            z = zpad[i + 1]
            az = d_ref[i] * z - neighbours(i, zpad, xl, xh, yl, yh)
            az_ref[i] = az
            zaz = zaz + fold(z * az)
            zap = zap + fold(z * ap_ref[i])
            if e_q is not None:
                q = s_ref[i] * az
                qpad[i + 1] = q
                low, high = pack(e_q, i, q, low, high)
                for index in range(NV):
                    parts[index] = parts[index] + fold(w_ref[index, i] * az)
        if e_q is not None:
            start_all(halo_copies(e_q))
        return zaz, zap, parts

    def steps(rz, zaz, zap, rz_old, pap_old, first):
        beta = jnp.where(first, 0.0, rz / rz_old)
        pap = zaz + beta * (2.0 * zap + beta * pap_old)
        return beta, pap, rz / pap

    def iteration(k, carry):
        rz_part, rz_old, pap_old = carry
        e_q, e_l = E_LOOP + 2 * k, E_LOOP + 1 + 2 * k
        zaz, zap, parts = image_pass(e_q)
        exchange(k, coefficient_row(parts) + scalar_row([rz_part, zaz, zap]))
        local_pass(e_q, lq, e_l)

        @pl.when(k == 0)
        def _():
            recv_all(g_copies)
            for place in range(5):
                in_order(rows_nb.at[place], gmat.at[place + 1])

        fresh_c, sums = exchanged(k)
        rz, zaz, zap = sums
        beta, pap, alpha = steps(rz, zaz, zap, rz_old, pap_old, k == 0)
        for place in range(6):
            yd = coarse_solution(gmat.at[place], fresh_c) + beta * yd_ref[place]
            yd_ref[place] = yd
            y_ref[place] = y_ref[place] - alpha * yd
        y_own = y_ref[0]
        rz_part = zero8
        for i in range(CZ):
            p = zpad[i + 1] + beta * p_ref[i]
            ap = az_ref[i] + beta * ap_ref[i]
            p_ref[i], ap_ref[i] = p, ap
            x_ref[i] = x_ref[i] + alpha * p
            r = r_ref[i] - alpha * ap
            r_ref[i] = r
            lqd = lq[i] + beta * lqp[i]
            lqp[i] = lqd
            z = lv[i] - alpha * lqd
            lv[i] = z
            for index in range(NV):
                z = z + w_ref[index, i] * y_own[index : index + 1, :]
            zpad[i + 1] = z
            rz_part = rz_part + fold(r * z)
        recv_all(halo_copies(e_l))
        for halo, old, base in ((hx, lqpx, lvx), (hy, lqpy, lvy)):
            for side in range(2):
                lqd = halo[e_l, side] + beta * old[side]
                old[side] = lqd
                base[side] = base[side] - alpha * lqd
        lqd = hz[e_l] + beta * lqpz[...]
        lqpz[...] = lqd
        lvz[...] = lvz[...] - alpha * lqd
        z_faces()
        return rz_part, rz, pap

    one = jnp.ones((1, 1), F32)
    rz_part, rz_old, pap_old = lax.fori_loop(0, ITERS - 1, iteration, (rz_first, one, one))
    zaz, zap, _ = image_pass(None)
    exchange(ITERS - 1, scalar_row([rz_part, zaz, zap]))
    _, sums = exchanged(ITERS - 1)
    beta, pap, alpha = steps(*sums, rz_old, pap_old, False)
    for i in range(CZ):
        p_ref[i] = alpha * (zpad[i + 1] + beta * p_ref[i])
        ap_ref[i] = alpha * (az_ref[i] + beta * ap_ref[i])

    for e in range(HALOS):
        send_all(halo_copies(e))
    for k in range(ITERS):
        pair_copy(k).wait_send()
        wide_all(k).wait_send()
        far_all(k).wait_send()
    send_all([a_all, b_all, own_all, rows_all] + w_copies + g_copies + y_copies)


def local(right_side, permeability, storage, deflation, coarse_inverse, owners, margin):
    hbm = pl.BlockSpec(memory_space=pltpu.HBM)
    vmem = pl.BlockSpec(memory_space=pltpu.VMEM)
    shape = jax.ShapeDtypeStruct((CZ, CX, CY), F32)
    dma = pltpu.SemaphoreType.DMA

    def ram(*dims, dtype=F32):
        return pltpu.VMEM(dims, dtype)

    field, padded = ram(CZ, CX, CY), ram(CZ + 2, CX, CY)
    plane, ends = ram(CX, CY), ram(2, 8, 128)
    before, rest, last_step, last_image = pl.pallas_call(
        kernel,
        out_shape=(shape,) * 4,
        in_specs=[hbm] * 7,
        out_specs=(vmem,) * 4,
        scratch_shapes=[
            field, field, ram(NV, CZ, CX, CY), ram(*coarse_inverse.shape),
            ram(*owners.shape, dtype=jnp.int32), ram(*margin.shape, dtype=jnp.int32),
            padded, padded, field, field, field, ram(CZ + 1, CX, CY),
            field, field, field, field, field, field, field,
            ram(HALOS, CX, CY), ram(HALOS, 2, 8, 128), ram(HALOS, 2, 8, 128),
            ram(HALOS, CX, CY), ram(HALOS, 2, 8, 128), ram(HALOS, 2, 8, 128),
            ends, ends, ends, ends, plane, ends, ends, plane, ends, ends,
            ram(NV, CX, CY), ram(2, NV, 8, 128), ram(2, NV, 8, 128), ram(2, NV, 8, 128), ram(2, NV, 8, 128),
            ram(GROUP, 2, 128), ram(GROUP, 2, 128), ram(ITERS, 2, 1, 128), ram(ITERS, 8, 128),
            ram(ITERS, CHIPS, 128), ram(ITERS, 2, CHIPS, 128),
            ram(GROUP, 8, 128), ram(GROUP, 8, 128), ram(GROUP, 8, 128), ram(5, GROUP, 8, 128),
            ram(6, GROUP, 8, 128), ram(3, *coarse_inverse.shape, dtype=jnp.bfloat16), ram(8, 128), ram(5, 8, 128), ram(6, 8, 128), ram(6, 8, 128),
            dma((7,)), dma((HALOS, 5)), dma((HALOS, 5)), dma, dma, dma, dma, dma((2,)), dma((2,)),
            dma((5,)), dma((5,)), dma((5,)), dma((5,)), dma((5,)), dma((5,)),
            dma((ITERS,)), dma((ITERS,)), dma((ITERS,)), dma((ITERS,)), dma((ITERS,)), dma((ITERS,)),
        ],
        compiler_params=pltpu.CompilerParams(
            collective_id=0, has_side_effects=True, vmem_limit_bytes=55312384
        ),
    )(right_side, permeability, storage, deflation, coarse_inverse, owners, margin)
    return before + last_step, rest - last_image


def solution(mesh):
    in_specs = (
        P("gz", "gx", "gy"),
        P("gz", "gx", "gy"),
        P("gz", "gx", "gy"),
        P(None, "gz", "gx", "gy"),
        P("gx", None),
        P("gz", "gx", "gy", None),
        P("gz", "gx", "gy", None),
    )
    out_specs = (P("gz", "gx", "gy"), P("gz", "gx", "gy"))
    return jax.shard_map(local, mesh=mesh, in_specs=in_specs, out_specs=out_specs, check_vma=False)
```
